32 devices in a mesh: req: 4 (over y, x), seq: 8 (over z, core).
Axes of the slice: x: 2, y: 2, z: 4, core: 2. Of those that a mesh axis runs over, the one named last changes fastest.
Arguments:
- new_tokens: bfloat16 [32, 4, 2048], P('req'), may hold values from -6 to 6
- norm_gain: float32 [2048], replicated, may hold values from 0.5 to 1.5
- w_query: bfloat16 [2048, 2048], P(None, 'req'), may hold values from -0.25 to 0.25
- w_key: bfloat16 [2048, 1024], P(None, 'req'), may hold values from -0.125 to 0.125
- w_value: bfloat16 [2048, 1024], P(None, 'req'), may hold values from -0.125 to 0.125
- w_out: bfloat16 [2048, 2048], P('req'), may hold values from -0.125 to 0.125
- pool_keys: bfloat16 [4096, 16, 1024], P(('req', 'seq')), may hold values from -1000 to 1000
- pool_values: bfloat16 [4096, 16, 1024], P(('req', 'seq')), may hold values from -6 to 6
- cache_lengths: int32 [32], replicated, may hold values from 2 to 2044, as said below
- owner: int32 [32], replicated, may hold values from 0 to 31, as said below
- page_table: int32 [32, 128], replicated, may hold values from 0 to 4095, as said below
Outputs:
- out_hidden: bfloat16 [32, 4, 2048], P('req')
- keys_out: bfloat16 [32, 2048, 1024], P('req', 'seq')
- values_out: bfloat16 [32, 2048, 1024], P('req', 'seq')
The draws below stay inside these ranges and needn't reach their ends.
Inputs may be any that keep to these rules, and one draw needn't show every extreme that they name: A permutation: request r goes to owner slot owner[r], held by request group owner[r] // 8. page_table[r, j] is the pool page holding positions j * 16 to (j + 1) * 16 - 1 of request r; every pool page is named exactly once. Pool pages d * 128 to (d + 1) * 128 - 1 lie on device d of req+seq. The home of page j of request r is the device with req index owner[r] // 8 and seq index j // 16; every device's pool pages include exactly 4 pages of every home. `cache_lengths`: 2044 is reached in every draw.
All inputs are finite; a program needn't handle non-finite values.
Results may differ from the reference program's by a relative error of at most 0.015.
Values may be sent and summed in bfloat16 or wider, within the bound.
A program may use at most 128 MiB of HBM per device.

```python
import math
import jax
import jax.numpy as jnp
from jax import lax

D = 2048
H = 16
KVH = 8
HD = 128
NEW = 4
PAGE = 16
R_DEV = 8
REQS = 32
L_MAX = 2048
PPD = 16
PPR = 128
PAGES_DEV = 128
PER_PEER = 4
POOL = 4096
QW = 2048
KVW = 1024


def route_tables(key):
    devices = POOL // PAGES_DEV
    seq_count = PPR // PPD
    first_key = jax.random.fold_in(key, 101)
    spread_key = jax.random.fold_in(key, 102)
    shuffle_key = jax.random.fold_in(key, 103)
    owners = jax.random.permutation(first_key, REQS).astype(jnp.int32)
    spread = jax.vmap(lambda single: jax.random.permutation(single, PAGES_DEV))(jax.random.split(spread_key, devices)).astype(jnp.int32)
    shuffle = jax.vmap(lambda single: jax.random.permutation(single, PAGES_DEV))(jax.random.split(shuffle_key, devices)).astype(jnp.int32)
    home_dev = jnp.arange(devices, dtype=jnp.int32)[:, None]
    source = (home_dev + spread) % devices
    position = home_dev * PER_PEER + spread // devices
    local_slot = shuffle[source, position]
    slot_table = source * PAGES_DEV + local_slot
    owner_col = owners[:, None]
    logical = jnp.arange(PPR, dtype=jnp.int32)[None, :]
    home_row = owner_col // R_DEV * seq_count + logical // PPD
    home_col = owner_col % R_DEV * PPD + logical % PPD
    return (owners, slot_table[home_row, home_col].astype(jnp.int32))


def draw_owner(key, part):
    return route_tables(key)[0]


def draw_page_table(key, part):
    return route_tables(key)[1]


def draw_cache_lengths(key, part):
    longest = L_MAX - NEW
    drawn_lengths = jax.random.randint(jax.random.fold_in(key, 201), (REQS,), 2, longest + 1)
    chosen = jax.random.randint(jax.random.fold_in(key, 202), (), 0, REQS)
    return jnp.where(jnp.arange(REQS) == chosen, longest, drawn_lengths).astype(jnp.int32)


def draw_pool_keys(key, part):
    shape_all = (POOL, PAGE, KVW)
    values = 1.5 * jnp.clip(jax.random.normal(jax.random.fold_in(key, 304), shape_all, jnp.float32), -6.0, 6.0)
    return values.astype(jnp.bfloat16)


def shard_levels(own_key, dims, shards, smallest, largest):
    factor_of = 1.0
    for dim, parts in shards:
        draws = jax.random.uniform(jax.random.fold_in(jax.random.fold_in(own_key, 6), dim), (parts,), jnp.float32, smallest / len(shards), largest / len(shards))
        factor_of = factor_of * jnp.repeat(jnp.exp(draws), dims[dim] // parts).reshape((-1,) + (1,) * (len(dims) - 1 - dim))
    return factor_of


def centred(stream_key, shape, scale, most, shards=(), held_as=jnp.bfloat16):
    entries = jax.random.normal(stream_key, shape, jnp.float32) * scale
    if len(shards) > 0:
        entries = shard_levels(stream_key, shape, shards, -0.22, 0.18) * entries
    return jnp.clip(entries, min=-most, max=most).astype(held_as)


def setup_inputs(seed: int = 0) -> dict:
    keys = jax.random.split(jax.random.key(seed), 12)
    return {
        "new_tokens": centred(keys[0], (REQS, NEW, D), 1.0, 6.0, ((0, 4),)),
        "norm_gain": jnp.clip(1.0 + 0.1 * jax.random.normal(keys[1], (D,), jnp.float32), 0.5, 1.5),
        "w_query": centred(keys[2], (D, QW), (D // 4) ** -0.5, 0.25, ((1, 4),)),
        "w_key": centred(keys[3], (D, KVW), D ** -0.5, 0.125, ((1, 4),)),
        "w_value": centred(keys[4], (D, KVW), D ** -0.5, 0.125, ((1, 4),)),
        "w_out": centred(keys[5], (QW, D), QW ** -0.5, 0.125, ((0, 4),)),
        "pool_keys": draw_pool_keys(jax.random.fold_in(keys[11], 71), 0),
        "pool_values": centred(keys[7], (POOL, PAGE, KVW), 1.0, 6.0, ((0, 32),)),
        "cache_lengths": draw_cache_lengths(jax.random.fold_in(keys[11], 71), 0),
        "owner": draw_owner(jax.random.fold_in(keys[11], 71), 0),
        "page_table": draw_page_table(jax.random.fold_in(keys[11], 71), 0),
    }


NORM_EPS = 1e-05
ROPE_BASE = 1000000.0
MASKED = -1e+30

def rotate(values, places):
    half_dim = values.shape[-1] // 2
    steps_up = jnp.arange(half_dim, dtype=jnp.float32) * (2.0 / values.shape[-1])
    inverse = ROPE_BASE ** (-steps_up)
    angles = places.astype(jnp.float32)[..., None] * inverse
    cosine = jnp.cos(angles)[..., None, :]
    sine_part = jnp.sin(angles)[..., None, :]
    first_half = values[..., :half_dim]
    second_half = values[..., half_dim:]
    return jnp.concatenate([first_half * cosine - second_half * sine_part, second_half * cosine + first_half * sine_part], axis=-1)

def reference(new_tokens, norm_gain, w_query, w_key, w_value, w_out, pool_keys, pool_values, cache_lengths, owner, page_table):
    groups = H // KVH
    slot_request = jnp.zeros((REQS,), jnp.int32).at[owner].set(jnp.arange(REQS, dtype=jnp.int32))
    slot_lengths = cache_lengths[slot_request]
    slot_pages = page_table[slot_request]
    tokens_wide = new_tokens.astype(jnp.float32)
    square_mean = lax.optimization_barrier(jnp.mean(tokens_wide * tokens_wide, axis=-1, keepdims=True))
    normed = (tokens_wide * lax.rsqrt(square_mean + NORM_EPS) * norm_gain.astype(jnp.float32)).astype(jnp.bfloat16)
    flat_rows = normed.reshape(REQS * NEW, D)
    places = slot_lengths[:, None] + jnp.arange(NEW, dtype=jnp.int32)[None, :]
    queries = jnp.dot(flat_rows, w_query, preferred_element_type=jnp.float32).reshape(REQS, NEW, H, HD)
    fresh_keys = jnp.dot(flat_rows, w_key, preferred_element_type=jnp.float32).reshape(REQS, NEW, KVH, HD)
    fresh_values = jnp.dot(flat_rows, w_value, preferred_element_type=jnp.float32).reshape(REQS, NEW, KVH, HD)
    queries = rotate(queries, places).astype(jnp.bfloat16)
    fresh_keys = rotate(fresh_keys, places).astype(jnp.bfloat16)
    fresh_values = fresh_values.astype(jnp.bfloat16)
    score_scale = 1.0 / math.sqrt(HD)
    key_pos = jnp.arange(L_MAX + NEW, dtype=jnp.int32)
    new_index = jnp.arange(NEW, dtype=jnp.int32)

    def attend(packed):
        page_rows, length, query_one, keys_one, values_one = packed
        cached_keys = pool_keys[page_rows].reshape(L_MAX, KVW)
        cached_values = pool_values[page_rows].reshape(L_MAX, KVW)
        all_keys = jnp.concatenate([cached_keys, keys_one.reshape(NEW, KVW)], axis=0).reshape(L_MAX + NEW, KVH, HD).astype(jnp.float32)
        all_values = jnp.concatenate([cached_values, values_one.reshape(NEW, KVW)], axis=0).reshape(L_MAX + NEW, KVH, HD).astype(jnp.float32)
        grouped = query_one.reshape(NEW, KVH, groups, HD).astype(jnp.float32)
        scores = jnp.einsum('tkgd,pkd->kgtp', grouped, all_keys) * score_scale
        visible = jnp.where(key_pos[None, :] < L_MAX, key_pos[None, :] < length, key_pos[None, :] - L_MAX <= new_index[:, None])
        scores = jnp.where(visible, scores, MASKED)
        row_peak = lax.optimization_barrier(jnp.max(scores, axis=-1, keepdims=True))
        weights = jnp.where(visible, jnp.exp(scores - row_peak), 0.0)
        denominator = lax.optimization_barrier(jnp.sum(weights, axis=-1))
        rounded = lax.optimization_barrier(weights.astype(jnp.bfloat16)).astype(jnp.float32)
        weighted = jnp.einsum('kgtp,pkd->tkgd', rounded, all_values)
        attended = (weighted / jnp.transpose(denominator, (2, 0, 1))[..., None]).reshape(NEW, QW).astype(jnp.bfloat16)
        keys_done = lax.dynamic_update_slice(cached_keys, keys_one.reshape(NEW, KVW), (length, jnp.int32(0)))
        values_done = lax.dynamic_update_slice(cached_values, values_one.reshape(NEW, KVW), (length, jnp.int32(0)))
        return (attended, keys_done, values_done)
    attention, keys_out, values_out = lax.map(attend, (slot_pages, slot_lengths, queries, fresh_keys, fresh_values))
    mixed_out = jnp.dot(attention.reshape(REQS * NEW, QW), w_out, preferred_element_type=jnp.float32).reshape(REQS, NEW, D)
    out_hidden = (tokens_wide + mixed_out).astype(jnp.bfloat16)
    return (out_hidden, keys_out, values_out)
```

```python
import functools
import math

import jax
import jax.numpy as jnp
from jax import lax
from jax.experimental import pallas as pl
from jax.experimental.pallas import tpu as pltpu
from jax.sharding import PartitionSpec as P

H = 16
KVH = 8
HD = 128
GROUPS = H // KVH

NORM_EPS = 1e-05
ROPE_BASE = 1000000.0
MASKED = -1e30
VMEM_BYTES = 48 * 1024 * 1024


def rotate(values, places):
    half_dim = values.shape[-1] // 2
    steps_up = jnp.arange(half_dim, dtype=jnp.float32) * (2.0 / values.shape[-1])
    inverse = ROPE_BASE ** (-steps_up)
    angles = places.astype(jnp.float32)[..., None] * inverse
    cosine = jnp.cos(angles)[..., None, :]
    sine_part = jnp.sin(angles)[..., None, :]
    first_half = values[..., :half_dim]
    second_half = values[..., half_dim:]
    return jnp.concatenate(
        [
            first_half * cosine - second_half * sine_part,
            second_half * cosine + first_half * sine_part,
        ],
        axis=-1,
    )


def attend_kernel(
    new_count, page_info, own_info, q_ref, k_ref, v_ref, kn_ref, vn_ref, acc_ref, max_ref, sum_ref
):
    scale = 1.0 / math.sqrt(HD)
    q = q_ref[0]
    rows = q.shape[0]
    dims = (((1,), (1,)), ((), ()))
    scores = lax.dot_general(q, k_ref[...], dims, preferred_element_type=jnp.float32) * scale
    own = lax.dot_general(q, kn_ref[0], dims, preferred_element_type=jnp.float32) * scale
    row_ids = lax.broadcasted_iota(jnp.int32, (rows, 1), 0)
    row_slot = row_ids // (GROUPS * new_count)
    row_token = row_ids % new_count
    live = page_info[...] == row_slot
    own_token = lax.broadcasted_iota(jnp.int32, own.shape, 1) % new_count
    own_live = (own_info[...] == row_slot) & (own_token <= row_token)
    scores = jnp.where(live, scores, MASKED)
    own = jnp.where(own_live, own, MASKED)
    peak = jnp.maximum(
        jnp.max(scores, axis=-1, keepdims=True), jnp.max(own, axis=-1, keepdims=True)
    )
    weights = jnp.where(live, jnp.exp(scores - peak), 0.0)
    own_weights = jnp.where(own_live, jnp.exp(own - peak), 0.0)
    mass = jnp.sum(weights, axis=-1, keepdims=True) + jnp.sum(own_weights, axis=-1, keepdims=True)
    acc_ref[0] = jnp.dot(
        weights.astype(jnp.bfloat16), v_ref[...], preferred_element_type=jnp.float32
    ) + jnp.dot(own_weights.astype(jnp.bfloat16), vn_ref[0], preferred_element_type=jnp.float32)
    max_ref[0] = peak
    sum_ref[0] = mass


def attend(page_info, own_info, queries, keys, values, keys_new, values_new, new_count):
    rows = queries.shape[1]
    spots = keys.shape[0]
    own = keys_new.shape[1]
    whole = lambda shape: pl.BlockSpec(shape, lambda h: (0, 0))
    per_head = lambda shape: pl.BlockSpec((1,) + shape, lambda h: (h, 0, 0))
    return pl.pallas_call(
        functools.partial(attend_kernel, new_count),
        grid=(KVH,),
        in_specs=[
            whole((1, spots)),
            whole((1, own)),
            per_head((rows, HD)),
            pl.BlockSpec((spots, HD), lambda h: (0, h)),
            pl.BlockSpec((spots, HD), lambda h: (0, h)),
            per_head((own, HD)),
            per_head((own, HD)),
        ],
        out_specs=[per_head((rows, HD)), per_head((rows, 1)), per_head((rows, 1))],
        out_shape=[
            jax.ShapeDtypeStruct((KVH, rows, HD), jnp.float32),
            jax.ShapeDtypeStruct((KVH, rows, 1), jnp.float32),
            jax.ShapeDtypeStruct((KVH, rows, 1), jnp.float32),
        ],
        compiler_params=pltpu.CompilerParams(vmem_limit_bytes=VMEM_BYTES),
        cost_estimate=pl.CostEstimate(
            flops=4 * KVH * rows * spots * HD,
            bytes_accessed=4 * KVH * spots * HD,
            transcendentals=KVH * rows * spots,
        ),
        name="attend_held_pages",
    )(page_info, own_info, queries, keys, values, keys_new, values_new)


def place_kernel(placement, starts, fresh, incoming, out, buf, in_sems, out_sems):
    slots, new_count, _ = fresh.shape
    pages, page_len, _ = buf.shape
    per_slot = pages // slots
    for slot in range(slots):
        for step in range(per_slot):
            page = slot * per_slot + step
            pltpu.make_async_copy(
                incoming.at[placement[page]], buf.at[page], in_sems.at[slot]
            ).start()
    for slot in range(slots):
        mine = pl.ds(slot * per_slot, per_slot)
        pltpu.make_async_copy(incoming.at[mine], buf.at[mine], in_sems.at[slot]).wait()
        for token in range(new_count):
            spot = starts[slot] + token

            @pl.when((spot >= 0) & (spot < per_slot * page_len))
            def _():
                page = slot * per_slot + spot // page_len
                block = buf[page].astype(jnp.float32)
                here = lax.broadcasted_iota(jnp.int32, block.shape, 0) == spot % page_len
                row = fresh[slot, pl.ds(token, 1), :]
                buf[page] = jnp.where(here, row, block).astype(buf.dtype)

        pltpu.make_async_copy(buf.at[mine], out.at[mine], out_sems.at[slot]).start()
    for slot in range(slots):
        mine = pl.ds(slot * per_slot, per_slot)
        pltpu.make_async_copy(buf.at[mine], out.at[mine], out_sems.at[slot]).wait()


def place(placement, starts, fresh, incoming, name):
    slots = fresh.shape[0]
    smem = pl.BlockSpec(memory_space=pltpu.SMEM)
    return pl.pallas_call(
        place_kernel,
        in_specs=[
            smem,
            smem,
            pl.BlockSpec(memory_space=pltpu.VMEM),
            pl.BlockSpec(memory_space=pl.ANY),
        ],
        out_specs=pl.BlockSpec(memory_space=pl.ANY),
        out_shape=jax.ShapeDtypeStruct(incoming.shape, incoming.dtype),
        scratch_shapes=[
            pltpu.VMEM(incoming.shape, incoming.dtype),
            pltpu.SemaphoreType.DMA((slots,)),
            pltpu.SemaphoreType.DMA((slots,)),
        ],
        compiler_params=pltpu.CompilerParams(vmem_limit_bytes=VMEM_BYTES),
        cost_estimate=pl.CostEstimate(
            flops=0, bytes_accessed=2 * incoming.size * 2, transcendentals=0
        ),
        name=name,
    )(placement, starts, fresh, incoming)


def shards(
    new_tokens,
    norm_gain,
    w_query,
    w_key,
    w_value,
    w_out,
    pool_keys,
    pool_values,
    cache_lengths,
    owner,
    page_table,
):
    req_count = lax.axis_size("req")
    seq_count = lax.axis_size("seq")
    devices = req_count * seq_count
    req_index = lax.axis_index("req")
    seq_index = lax.axis_index("seq")
    device_index = req_index * seq_count + seq_index
    local_reqs, new_count, model_width = new_tokens.shape
    slot_total = owner.shape[0]
    pages_dev, page_len, kv_width = pool_keys.shape
    pages_req = page_table.shape[1]
    pages_home = pages_req // seq_count
    positions = pages_home * page_len
    per_peer = pages_dev // devices
    query_cols = w_query.shape[1]
    key_cols = w_key.shape[1]
    i32 = jnp.int32
    local_pages = jnp.arange(pages_dev, dtype=i32)

    logical = jnp.arange(pages_req, dtype=i32)[None, :]
    home_index = (
        (owner[:, None] // local_reqs * seq_count + logical // pages_home) * pages_dev
        + owner[:, None] % local_reqs * pages_home
        + logical % pages_home
    )
    held = page_table[None] == (device_index * pages_dev + local_pages)[:, None, None]
    held_homes = jnp.sum(jnp.where(held, home_index[None], 0), axis=(1, 2))
    send_rank = jnp.sum((held_homes[None, :] < held_homes[:, None]).astype(i32), axis=1)
    send_order = jnp.sum(
        jnp.where(send_rank[None, :] == local_pages[:, None], local_pages[None, :], 0), axis=1
    )

    def move(pool):
        outgoing = pool.at[send_order].get(mode="promise_in_bounds")
        outgoing = outgoing.reshape(devices, per_peer, page_len, kv_width)
        incoming = lax.all_to_all(outgoing, ("req", "seq"), split_axis=0, concat_axis=0, tiled=True)
        return incoming.reshape(pages_dev, page_len, kv_width)

    in_keys = move(pool_keys)
    in_values = move(pool_values)

    slots = jnp.arange(slot_total, dtype=i32)
    slot_owned = owner[None, :] == slots[:, None]
    slot_request = jnp.sum(jnp.where(slot_owned, slots[None, :], 0), axis=1)
    slot_lengths = jnp.sum(jnp.where(slot_owned, cache_lengths[None, :], 0), axis=1)
    my_requests = lax.dynamic_slice_in_dim(slot_request, req_index * local_reqs, local_reqs)
    my_lengths = lax.dynamic_slice_in_dim(slot_lengths, req_index * local_reqs, local_reqs)
    seq_pages = lax.dynamic_slice_in_dim(page_table, seq_index * pages_home, pages_home, axis=1)
    is_mine = my_requests[:, None, None] == slots[None, :, None]
    source = jnp.sum(jnp.where(is_mine, seq_pages[None], 0), axis=1).reshape(-1) // pages_dev
    ahead = (source[None, :] == source[:, None]) & (local_pages[None, :] < local_pages[:, None])
    placement = source * per_peer + jnp.sum(ahead.astype(i32), axis=1)

    tokens_wide = new_tokens.astype(jnp.float32)
    square_mean = jnp.mean(tokens_wide * tokens_wide, axis=-1, keepdims=True)
    normed = (tokens_wide * lax.rsqrt(square_mean + NORM_EPS) * norm_gain).astype(jnp.bfloat16)
    flat_rows = lax.all_gather(
        normed.reshape(local_reqs * new_count, model_width), "req", axis=0, tiled=True
    )
    new_index = jnp.arange(new_count, dtype=i32)
    places = slot_lengths[:, None] + new_index[None, :]
    heads = lambda w: jnp.dot(flat_rows, w, preferred_element_type=jnp.float32)
    queries_now = heads(w_query).reshape(slot_total, new_count, query_cols // HD, HD)
    keys_now = heads(w_key).reshape(slot_total, new_count, key_cols // HD, HD)
    queries_now = rotate(queries_now, places).reshape(slot_total * new_count, query_cols)
    keys_now = rotate(keys_now, places).reshape(slot_total * new_count, key_cols)
    projected = jnp.concatenate([queries_now, keys_now, heads(w_value)], axis=-1)
    every = lax.all_gather(projected.astype(jnp.bfloat16), "req", axis=0, tiled=False)
    own_kv = key_cols // HD
    queries = every[..., :query_cols].reshape(
        req_count, slot_total, new_count, own_kv, GROUPS, HD
    )
    queries = jnp.transpose(queries, (0, 3, 1, 4, 2, 5)).reshape(KVH, -1, HD)

    def by_head(part):
        part = part.reshape(req_count, slot_total * new_count, own_kv, HD)
        return jnp.transpose(part, (0, 2, 1, 3)).reshape(KVH, slot_total * new_count, HD)

    def of_mine(part):
        part = part.reshape(req_count, slot_total, new_count, key_cols)
        part = lax.dynamic_slice_in_dim(part, req_index * local_reqs, local_reqs, axis=1)
        part = jnp.transpose(part, (1, 2, 0, 3)).reshape(local_reqs, new_count, kv_width)
        return part.astype(jnp.float32)

    new_keys = every[..., query_cols : query_cols + key_cols]
    new_values = every[..., query_cols + key_cols :]

    held_dev = held_homes // pages_dev
    held_slot = held_dev // seq_count * local_reqs + held_homes % pages_dev // pages_home
    held_first = (held_dev % seq_count * pages_home + held_homes % pages_home) * page_len
    held_length = jnp.sum(
        jnp.where(held_slot[:, None] == slots[None, :], slot_lengths[None, :], 0), axis=1
    )
    spots = held_first[:, None] + jnp.arange(page_len, dtype=i32)[None, :]
    page_info = jnp.where(spots < held_length[:, None], held_slot[:, None], -1).reshape(1, -1)
    own_info = jnp.where(device_index == 0, jnp.repeat(slots, new_count), -1).reshape(1, -1)
    total, peak, mass = attend(
        page_info,
        own_info,
        queries,
        pool_keys.reshape(pages_dev * page_len, kv_width),
        pool_values.reshape(pages_dev * page_len, kv_width),
        by_head(new_keys),
        by_head(new_values),
        new_count,
    )
    peak = peak[..., 0]
    mass = mass[..., 0]
    rows = peak.shape[1]
    rescale = jnp.exp(peak - lax.pmax(peak, ("req", "seq")))
    packed = jnp.concatenate(
        [total * rescale[..., None], (mass * rescale).reshape(KVH, rows // HD, HD)], axis=1
    ).astype(jnp.bfloat16)
    packed = lax.psum(packed, ("req", "seq"))
    packed = lax.dynamic_slice_in_dim(packed, req_index * own_kv, own_kv).astype(jnp.float32)
    attended = packed[:, :rows] / packed[:, rows:].reshape(own_kv, rows, 1)
    attended = attended.reshape(own_kv, slot_total, GROUPS, new_count, HD)
    attended = (
        jnp.transpose(attended, (1, 3, 0, 2, 4))
        .reshape(slot_total * new_count, query_cols)
        .astype(jnp.bfloat16)
    )
    shares = jnp.dot(attended, w_out, preferred_element_type=jnp.float32).astype(jnp.bfloat16)
    summed = lax.psum_scatter(shares, "req", scatter_dimension=0, tiled=True).astype(jnp.float32)
    out_hidden = (tokens_wide + summed.reshape(tokens_wide.shape)).astype(jnp.bfloat16)

    starts = my_lengths - seq_index * positions
    out_shape = (local_reqs, positions, kv_width)
    keys_out = place(placement, starts, of_mine(new_keys), in_keys, "place_keys")
    values_out = place(placement, starts, of_mine(new_values), in_values, "place_values")
    return (out_hidden, keys_out.reshape(out_shape), values_out.reshape(out_shape))


def solution(mesh):
    return jax.shard_map(
        shards,
        mesh=mesh,
        in_specs=(
            P("req", None, None),
            P(),
            P(None, "req"),
            P(None, "req"),
            P(None, "req"),
            P("req", None),
            P(("req", "seq"), None, None),
            P(("req", "seq"), None, None),
            P(),
            P(),
            P(),
        ),
        out_specs=(P("req", None, None), P("req", "seq", None), P("req", "seq", None)),
        check_vma=False,
    )
```

```python
import functools
import math

import jax
import jax.numpy as jnp
from jax import lax
from jax.experimental import pallas as pl
from jax.experimental.pallas import tpu as pltpu
from jax.sharding import PartitionSpec as P

H = 16
KVH = 8
HD = 128
GROUPS = H // KVH

NORM_EPS = 1e-05
ROPE_BASE = 1000000.0
MASKED = -1e30
VMEM_BYTES = 48 * 1024 * 1024


def rotate(values, places):
    half_dim = values.shape[-1] // 2
    steps_up = jnp.arange(half_dim, dtype=jnp.float32) * (2.0 / values.shape[-1])
    inverse = ROPE_BASE ** (-steps_up)
    angles = places.astype(jnp.float32)[..., None] * inverse
    cosine = jnp.cos(angles)[..., None, :]
    sine_part = jnp.sin(angles)[..., None, :]
    first_half = values[..., :half_dim]
    second_half = values[..., half_dim:]
    return jnp.concatenate(
        [
            first_half * cosine - second_half * sine_part,
            second_half * cosine + first_half * sine_part,
        ],
        axis=-1,
    )


def attend_kernel(
    new_count, page_info, own_info, q_ref, k_ref, v_ref, kn_ref, vn_ref, acc_ref, max_ref, sum_ref
):
    scale = 1.0 / math.sqrt(HD)
    q = q_ref[0]
    rows = q.shape[0]
    dims = (((1,), (1,)), ((), ()))
    scores = lax.dot_general(q, k_ref[...], dims, preferred_element_type=jnp.float32) * scale
    own = lax.dot_general(q, kn_ref[0], dims, preferred_element_type=jnp.float32) * scale
    row_ids = lax.broadcasted_iota(jnp.int32, (rows, 1), 0)
    row_slot = row_ids // (GROUPS * new_count)
    row_token = row_ids % new_count
    live = page_info[...] == row_slot
    own_token = lax.broadcasted_iota(jnp.int32, own.shape, 1) % new_count
    own_live = (own_info[...] == row_slot) & (own_token <= row_token)
    scores = jnp.where(live, scores, MASKED)
    own = jnp.where(own_live, own, MASKED)
    peak = jnp.maximum(
        jnp.max(scores, axis=-1, keepdims=True), jnp.max(own, axis=-1, keepdims=True)
    )
    weights = jnp.where(live, jnp.exp(scores - peak), 0.0)
    own_weights = jnp.where(own_live, jnp.exp(own - peak), 0.0)
    mass = jnp.sum(weights, axis=-1, keepdims=True) + jnp.sum(own_weights, axis=-1, keepdims=True)
    acc_ref[0] = jnp.dot(
        weights.astype(jnp.bfloat16), v_ref[...], preferred_element_type=jnp.float32
    ) + jnp.dot(own_weights.astype(jnp.bfloat16), vn_ref[0], preferred_element_type=jnp.float32)
    max_ref[0] = peak
    sum_ref[0] = mass


def attend(page_info, own_info, queries, keys, values, keys_new, values_new, new_count):
    rows = queries.shape[1]
    spots = keys.shape[0]
    own = keys_new.shape[1]
    whole = lambda shape: pl.BlockSpec(shape, lambda h: (0, 0))
    per_head = lambda shape: pl.BlockSpec((1,) + shape, lambda h: (h, 0, 0))
    return pl.pallas_call(
        functools.partial(attend_kernel, new_count),
        grid=(KVH,),
        in_specs=[
            whole((1, spots)),
            whole((1, own)),
            per_head((rows, HD)),
            pl.BlockSpec((spots, HD), lambda h: (0, h)),
            pl.BlockSpec((spots, HD), lambda h: (0, h)),
            per_head((own, HD)),
            per_head((own, HD)),
        ],
        out_specs=[per_head((rows, HD)), per_head((rows, 1)), per_head((rows, 1))],
        out_shape=[
            jax.ShapeDtypeStruct((KVH, rows, HD), jnp.float32),
            jax.ShapeDtypeStruct((KVH, rows, 1), jnp.float32),
            jax.ShapeDtypeStruct((KVH, rows, 1), jnp.float32),
        ],
        compiler_params=pltpu.CompilerParams(vmem_limit_bytes=VMEM_BYTES),
        cost_estimate=pl.CostEstimate(
            flops=4 * KVH * rows * spots * HD,
            bytes_accessed=4 * KVH * spots * HD,
            transcendentals=KVH * rows * spots,
        ),
        name="attend_held_pages",
    )(page_info, own_info, queries, keys, values, keys_new, values_new)


def collect_kernel(order, keys, values, out, buf, in_sems, out_sems):
    parts = in_sems.shape[0]
    devices, _, per_peer = buf.shape[:3]
    per_part = devices // parts
    for part in range(parts):
        for peer in range(part * per_part, (part + 1) * per_part):
            for step in range(per_peer):
                page = order[peer * per_peer + step]
                for kind, pool in enumerate((keys, values)):
                    pltpu.make_async_copy(
                        pool.at[page], buf.at[peer, kind, step], in_sems.at[part]
                    ).start()
    for part in range(parts):
        mine = pl.ds(part * per_part, per_part)
        pltpu.make_async_copy(out.at[mine], buf.at[mine], in_sems.at[part]).wait()
        pltpu.make_async_copy(buf.at[mine], out.at[mine], out_sems.at[part]).start()
    for part in range(parts):
        mine = pl.ds(part * per_part, per_part)
        pltpu.make_async_copy(buf.at[mine], out.at[mine], out_sems.at[part]).wait()


def collect(order, keys, values, devices):
    pages, page_len, width = keys.shape
    shape = (devices, 2, pages // devices, page_len, width)
    parts = 16
    whole = pl.BlockSpec(memory_space=pl.ANY)
    return pl.pallas_call(
        collect_kernel,
        in_specs=[pl.BlockSpec(memory_space=pltpu.SMEM), whole, whole],
        out_specs=whole,
        out_shape=jax.ShapeDtypeStruct(shape, keys.dtype),
        scratch_shapes=[
            pltpu.VMEM(shape, keys.dtype),
            pltpu.SemaphoreType.DMA((parts,)),
            pltpu.SemaphoreType.DMA((parts,)),
        ],
        compiler_params=pltpu.CompilerParams(vmem_limit_bytes=VMEM_BYTES),
        cost_estimate=pl.CostEstimate(
            flops=0, bytes_accessed=8 * keys.size, transcendentals=0
        ),
        name="collect_pages",
    )(order, keys, values)


def place_kernel(
    placement, starts, fresh_keys, fresh_values, incoming, out_keys, out_values, buf, in_sems, out_sems
):
    slots, new_count, _ = fresh_keys.shape
    _, pages, page_len, _ = buf.shape
    per_slot = pages // slots
    for slot in range(slots):
        for step in range(per_slot):
            page = slot * per_slot + step
            for kind in range(2):
                pltpu.make_async_copy(
                    incoming.at[placement[kind * pages + page]],
                    buf.at[kind, page],
                    in_sems.at[kind, slot],
                ).start()
    for slot in range(slots):
        mine = pl.ds(slot * per_slot, per_slot)
        for kind, (fresh, out) in enumerate(((fresh_keys, out_keys), (fresh_values, out_values))):
            pltpu.make_async_copy(out.at[mine], buf.at[kind, mine], in_sems.at[kind, slot]).wait()
            for token in range(new_count):
                spot = starts[slot] + token

                @pl.when((spot >= 0) & (spot < per_slot * page_len))
                def _():
                    page = slot * per_slot + spot // page_len
                    block = buf[kind, page].astype(jnp.float32)
                    here = lax.broadcasted_iota(jnp.int32, block.shape, 0) == spot % page_len
                    row = fresh[slot, pl.ds(token, 1), :]
                    buf[kind, page] = jnp.where(here, row, block).astype(buf.dtype)

            pltpu.make_async_copy(buf.at[kind, mine], out.at[mine], out_sems.at[kind, slot]).start()
    for slot in range(slots):
        mine = pl.ds(slot * per_slot, per_slot)
        for kind, out in enumerate((out_keys, out_values)):
            pltpu.make_async_copy(buf.at[kind, mine], out.at[mine], out_sems.at[kind, slot]).wait()


def place(placement, starts, fresh_keys, fresh_values, incoming):
    slots = fresh_keys.shape[0]
    pages = incoming.shape[0] // 2
    shape = (pages,) + incoming.shape[1:]
    smem = pl.BlockSpec(memory_space=pltpu.SMEM)
    vmem = pl.BlockSpec(memory_space=pltpu.VMEM)
    whole = pl.BlockSpec(memory_space=pl.ANY)
    return pl.pallas_call(
        place_kernel,
        in_specs=[smem, smem, vmem, vmem, whole],
        out_specs=[whole, whole],
        out_shape=[jax.ShapeDtypeStruct(shape, incoming.dtype)] * 2,
        scratch_shapes=[
            pltpu.VMEM((2,) + shape, incoming.dtype),
            pltpu.SemaphoreType.DMA((2, slots)),
            pltpu.SemaphoreType.DMA((2, slots)),
        ],
        compiler_params=pltpu.CompilerParams(vmem_limit_bytes=VMEM_BYTES),
        cost_estimate=pl.CostEstimate(
            flops=0, bytes_accessed=4 * incoming.size, transcendentals=0
        ),
        name="place_pages",
    )(placement, starts, fresh_keys, fresh_values, incoming)


def push_kernel(sizes, spread, count, *refs):
    srcs, outs = refs[:count], refs[count : 2 * count]
    send_sems, recv_sems = refs[2 * count :]
    total = math.prod(sizes.values())
    me = 0
    for name, size in sizes.items():
        me = me * size + lax.axis_index(name)

    def coords(flat):
        found = {}
        for name, size in reversed(sizes.items()):
            found[name] = lax.rem(flat, size)
            flat = lax.div(flat, size)
        return found

    barrier = pltpu.get_barrier_semaphore()

    def greet(step, _):
        peer = lax.rem(me + step, total)
        pl.semaphore_signal(
            barrier, inc=1, device_id=coords(peer), device_id_type=pl.DeviceIdType.MESH
        )
        return 0

    lax.fori_loop(1, total, greet, 0)
    pl.semaphore_wait(barrier, total - 1)

    def copy(which, step, place):
        peer = lax.rem(me + step, total)
        src = srcs[which].at[peer] if spread else srcs[which]
        return pltpu.make_async_remote_copy(
            src_ref=src,
            dst_ref=outs[which].at[place],
            send_sem=send_sems.at[which, step],
            recv_sem=recv_sems.at[which, step],
            device_id=coords(peer),
            device_id_type=pl.DeviceIdType.MESH,
        )

    def send(step, _):
        for which in range(count):
            copy(which, step, me).start()
        return 0

    lax.fori_loop(1, total, send, 0)
    for which in range(count):
        outs[which][me] = srcs[which][me] if spread else srcs[which][...]

    def finish(step, _):
        for which in range(count):
            copy(which, step, lax.rem(me + total - step, total)).wait_recv()
            copy(which, step, me).wait_send()
        return 0

    lax.fori_loop(1, total, finish, 0)


def push(arrays, axes, spread, collective_id, name):
    sizes = {axis: lax.axis_size(axis) for axis in axes}
    total = math.prod(sizes.values())
    vmem = pl.BlockSpec(memory_space=pltpu.VMEM)
    shapes = [a.shape if spread else (total,) + a.shape for a in arrays]
    return pl.pallas_call(
        functools.partial(push_kernel, sizes, spread, len(arrays)),
        in_specs=[vmem] * len(arrays),
        out_specs=[vmem] * len(arrays),
        out_shape=[jax.ShapeDtypeStruct(s, a.dtype) for s, a in zip(shapes, arrays)],
        scratch_shapes=[
            pltpu.SemaphoreType.DMA((len(arrays), total)),
            pltpu.SemaphoreType.DMA((len(arrays), total)),
        ],
        compiler_params=pltpu.CompilerParams(
            collective_id=collective_id, has_side_effects=True, vmem_limit_bytes=VMEM_BYTES // 2
        ),
        name=name,
    )(*arrays)


def shards(
    new_tokens,
    norm_gain,
    w_query,
    w_key,
    w_value,
    w_out,
    pool_keys,
    pool_values,
    cache_lengths,
    owner,
    page_table,
):
    req_count = lax.axis_size("req")
    seq_count = lax.axis_size("seq")
    devices = req_count * seq_count
    req_index = lax.axis_index("req")
    seq_index = lax.axis_index("seq")
    device_index = req_index * seq_count + seq_index
    local_reqs, new_count, model_width = new_tokens.shape
    slot_total = owner.shape[0]
    pages_dev, page_len, kv_width = pool_keys.shape
    pages_req = page_table.shape[1]
    pages_home = pages_req // seq_count
    positions = pages_home * page_len
    per_peer = pages_dev // devices
    query_cols = w_query.shape[1]
    key_cols = w_key.shape[1]
    i32 = jnp.int32
    local_pages = jnp.arange(pages_dev, dtype=i32)

    logical = jnp.arange(pages_req, dtype=i32)[None, :]
    home_index = (
        (owner[:, None] // local_reqs * seq_count + logical // pages_home) * pages_dev
        + owner[:, None] % local_reqs * pages_home
        + logical % pages_home
    )
    held = page_table[None] == (device_index * pages_dev + local_pages)[:, None, None]
    held_homes = jnp.sum(jnp.where(held, home_index[None], 0), axis=(1, 2))
    send_rank = jnp.sum((held_homes[None, :] < held_homes[:, None]).astype(i32), axis=1)
    send_order = jnp.sum(
        jnp.where(send_rank[None, :] == local_pages[:, None], local_pages[None, :], 0), axis=1
    )

    outgoing = collect(send_order, pool_keys, pool_values, devices)
    slots = jnp.arange(slot_total, dtype=i32)
    slot_owned = owner[None, :] == slots[:, None]
    slot_request = jnp.sum(jnp.where(slot_owned, slots[None, :], 0), axis=1)
    slot_lengths = jnp.sum(jnp.where(slot_owned, cache_lengths[None, :], 0), axis=1)
    my_requests = lax.dynamic_slice_in_dim(slot_request, req_index * local_reqs, local_reqs)
    my_lengths = lax.dynamic_slice_in_dim(slot_lengths, req_index * local_reqs, local_reqs)
    seq_pages = lax.dynamic_slice_in_dim(page_table, seq_index * pages_home, pages_home, axis=1)
    is_mine = my_requests[:, None, None] == slots[None, :, None]
    source = jnp.sum(jnp.where(is_mine, seq_pages[None], 0), axis=1).reshape(-1) // pages_dev
    ahead = (source[None, :] == source[:, None]) & (local_pages[None, :] < local_pages[:, None])
    placement = source * (2 * per_peer) + jnp.sum(ahead.astype(i32), axis=1)
    placement = jnp.concatenate([placement, placement + per_peer])

    tokens_wide = new_tokens.astype(jnp.float32)
    square_mean = jnp.mean(tokens_wide * tokens_wide, axis=-1, keepdims=True)
    normed = (tokens_wide * lax.rsqrt(square_mean + NORM_EPS) * norm_gain).astype(jnp.bfloat16)
    normed = normed.reshape(local_reqs * new_count, model_width)
    normed, outgoing = lax.optimization_barrier((normed, outgoing))
    incoming = lax.all_to_all(outgoing, ("req", "seq"), split_axis=0, concat_axis=0, tiled=True)
    incoming = incoming.reshape(2 * pages_dev, page_len, kv_width)
    flat_rows = push([normed], ("req",), False, 0, "gather_tokens")[0].reshape(-1, model_width)
    new_index = jnp.arange(new_count, dtype=i32)
    places = slot_lengths[:, None] + new_index[None, :]
    heads = lambda w: jnp.dot(flat_rows, w, preferred_element_type=jnp.float32)
    queries_now = heads(w_query).reshape(slot_total, new_count, query_cols // HD, HD)
    keys_now = heads(w_key).reshape(slot_total, new_count, key_cols // HD, HD)
    queries_now = rotate(queries_now, places).reshape(slot_total * new_count, query_cols)
    keys_now = rotate(keys_now, places).reshape(slot_total * new_count, key_cols)
    projected = jnp.concatenate([queries_now, keys_now, heads(w_value)], axis=-1)
    every = push([projected.astype(jnp.bfloat16)], ("req",), False, 1, "gather_heads")[0]
    own_kv = key_cols // HD
    queries = every[..., :query_cols].reshape(
        req_count, slot_total, new_count, own_kv, GROUPS, HD
    )
    queries = jnp.transpose(queries, (0, 3, 1, 4, 2, 5)).reshape(KVH, -1, HD)

    def by_head(part):
        part = part.reshape(req_count, slot_total * new_count, own_kv, HD)
        return jnp.transpose(part, (0, 2, 1, 3)).reshape(KVH, slot_total * new_count, HD)

    def of_mine(part):
        part = part.reshape(req_count, slot_total, new_count, key_cols)
        part = lax.dynamic_slice_in_dim(part, req_index * local_reqs, local_reqs, axis=1)
        part = jnp.transpose(part, (1, 2, 0, 3)).reshape(local_reqs, new_count, kv_width)
        return part.astype(jnp.float32)

    new_keys = every[..., query_cols : query_cols + key_cols]
    new_values = every[..., query_cols + key_cols :]

    held_dev = held_homes // pages_dev
    held_slot = held_dev // seq_count * local_reqs + held_homes % pages_dev // pages_home
    held_first = (held_dev % seq_count * pages_home + held_homes % pages_home) * page_len
    held_length = jnp.sum(
        jnp.where(held_slot[:, None] == slots[None, :], slot_lengths[None, :], 0), axis=1
    )
    spots = held_first[:, None] + jnp.arange(page_len, dtype=i32)[None, :]
    page_info = jnp.where(spots < held_length[:, None], held_slot[:, None], -1).reshape(1, -1)
    own_info = jnp.where(device_index == 0, jnp.repeat(slots, new_count), -1).reshape(1, -1)
    total, peak, mass = attend(
        page_info,
        own_info,
        queries,
        pool_keys.reshape(pages_dev * page_len, kv_width),
        pool_values.reshape(pages_dev * page_len, kv_width),
        by_head(new_keys),
        by_head(new_values),
        new_count,
    )
    peak = peak[..., 0]
    mass = mass[..., 0]
    seq_slots = slot_total // seq_count
    part_rows = seq_slots * GROUPS * new_count

    def by_device(part):
        part = part.reshape((req_count, own_kv, seq_count, part_rows) + part.shape[2:])
        part = jnp.swapaxes(part, 1, 2)
        return part.reshape((devices, own_kv * part_rows) + part.shape[4:])

    stats = jnp.stack([by_device(peak), by_device(mass)], axis=1)
    stats = jnp.pad(stats, ((0, 0), (0, 6), (0, HD - own_kv * part_rows)))
    parts, stats = push(
        [by_device(total).astype(jnp.bfloat16), stats], ("req", "seq"), True, 2, "share_partials"
    )
    peaks = stats[:, 0, : own_kv * part_rows]
    rescale = jnp.exp(peaks - jnp.max(peaks, axis=0))
    mass = jnp.sum(stats[:, 1, : own_kv * part_rows] * rescale, axis=0)
    attended = jnp.sum(parts.astype(jnp.float32) * rescale[..., None], axis=0) / mass[:, None]
    attended = push([attended.astype(jnp.bfloat16)], ("seq",), False, 3, "gather_slots")[0]
    attended = attended.reshape(seq_count, own_kv, seq_slots, GROUPS, new_count, HD)
    attended = jnp.transpose(attended, (0, 2, 4, 1, 3, 5)).reshape(-1, query_cols)
    shares = jnp.dot(attended, w_out, preferred_element_type=jnp.float32).astype(jnp.bfloat16)
    shares = shares.reshape(req_count, local_reqs * new_count, model_width)
    shares = push([shares], ("req",), True, 4, "share_outputs")[0]
    summed = jnp.sum(shares.astype(jnp.float32), axis=0)
    out_hidden = (tokens_wide + summed.reshape(tokens_wide.shape)).astype(jnp.bfloat16)

    starts = my_lengths - seq_index * positions
    out_shape = (local_reqs, positions, kv_width)
    keys_out, values_out = place(
        placement, starts, of_mine(new_keys), of_mine(new_values), incoming
    )
    return (out_hidden, keys_out.reshape(out_shape), values_out.reshape(out_shape))


def solution(mesh):
    return jax.shard_map(
        shards,
        mesh=mesh,
        in_specs=(
            P("req", None, None),
            P(),
            P(None, "req"),
            P(None, "req"),
            P(None, "req"),
            P("req", None),
            P(("req", "seq"), None, None),
            P(("req", "seq"), None, None),
            P(),
            P(),
            P(),
        ),
        out_specs=(P("req", None, None), P("req", "seq", None), P("req", "seq", None)),
        check_vma=False,
    )
```

```python
import functools
import math

import jax
import jax.numpy as jnp
from jax import lax
from jax.experimental import pallas as pl
from jax.experimental.pallas import tpu as pltpu
from jax.sharding import PartitionSpec as P

H = 16
KVH = 8
HD = 128
GROUPS = H // KVH

NORM_EPS = 1e-05
ROPE_BASE = 1000000.0
MASKED = -1e30
VMEM_BYTES = 48 * 1024 * 1024


def rotate(values, places):
    half_dim = values.shape[-1] // 2
    steps_up = jnp.arange(half_dim, dtype=jnp.float32) * (2.0 / values.shape[-1])
    inverse = ROPE_BASE ** (-steps_up)
    angles = places.astype(jnp.float32)[..., None] * inverse
    cosine = jnp.cos(angles)[..., None, :]
    sine_part = jnp.sin(angles)[..., None, :]
    first_half = values[..., :half_dim]
    second_half = values[..., half_dim:]
    return jnp.concatenate(
        [
            first_half * cosine - second_half * sine_part,
            second_half * cosine + first_half * sine_part,
        ],
        axis=-1,
    )


def attend_kernel(
    new_count, page_info, own_info, q_ref, k_ref, v_ref, kn_ref, vn_ref, acc_ref, max_ref, sum_ref
):
    scale = 1.0 / math.sqrt(HD)
    q = q_ref[0]
    rows = q.shape[0]
    dims = (((1,), (1,)), ((), ()))
    scores = lax.dot_general(q, k_ref[...], dims, preferred_element_type=jnp.float32) * scale
    own = lax.dot_general(q, kn_ref[0], dims, preferred_element_type=jnp.float32) * scale
    row_ids = lax.broadcasted_iota(jnp.int32, (rows, 1), 0)
    row_slot = row_ids // (GROUPS * new_count)
    row_token = row_ids % new_count
    live = page_info[...] == row_slot
    own_token = lax.broadcasted_iota(jnp.int32, own.shape, 1) % new_count
    own_live = (own_info[...] == row_slot) & (own_token <= row_token)
    scores = jnp.where(live, scores, MASKED)
    own = jnp.where(own_live, own, MASKED)
    peak = jnp.maximum(
        jnp.max(scores, axis=-1, keepdims=True), jnp.max(own, axis=-1, keepdims=True)
    )
    weights = jnp.where(live, jnp.exp(scores - peak), 0.0)
    own_weights = jnp.where(own_live, jnp.exp(own - peak), 0.0)
    mass = jnp.sum(weights, axis=-1, keepdims=True) + jnp.sum(own_weights, axis=-1, keepdims=True)
    acc_ref[0] = jnp.dot(
        weights.astype(jnp.bfloat16), v_ref[...], preferred_element_type=jnp.float32
    ) + jnp.dot(own_weights.astype(jnp.bfloat16), vn_ref[0], preferred_element_type=jnp.float32)
    max_ref[0] = peak
    sum_ref[0] = mass


def attend(page_info, own_info, queries, keys, values, keys_new, values_new, new_count):
    rows = queries.shape[1]
    spots = keys.shape[0]
    own = keys_new.shape[1]
    whole = lambda shape: pl.BlockSpec(shape, lambda h: (0, 0))
    per_head = lambda shape: pl.BlockSpec((1,) + shape, lambda h: (h, 0, 0))
    return pl.pallas_call(
        functools.partial(attend_kernel, new_count),
        grid=(KVH,),
        in_specs=[
            whole((1, spots)),
            whole((1, own)),
            per_head((rows, HD)),
            pl.BlockSpec((spots, HD), lambda h: (0, h)),
            pl.BlockSpec((spots, HD), lambda h: (0, h)),
            per_head((own, HD)),
            per_head((own, HD)),
        ],
        out_specs=[per_head((rows, HD)), per_head((rows, 1)), per_head((rows, 1))],
        out_shape=[
            jax.ShapeDtypeStruct((KVH, rows, HD), jnp.float32),
            jax.ShapeDtypeStruct((KVH, rows, 1), jnp.float32),
            jax.ShapeDtypeStruct((KVH, rows, 1), jnp.float32),
        ],
        compiler_params=pltpu.CompilerParams(vmem_limit_bytes=VMEM_BYTES),
        cost_estimate=pl.CostEstimate(
            flops=4 * KVH * rows * spots * HD,
            bytes_accessed=4 * KVH * spots * HD,
            transcendentals=KVH * rows * spots,
        ),
        name="attend_held_pages",
    )(page_info, own_info, queries, keys, values, keys_new, values_new)


def collect_kernel(order, keys, values, out, buf, in_sems, out_sems):
    parts = in_sems.shape[0]
    devices, _, per_peer = buf.shape[:3]
    per_part = devices // parts
    for part in range(parts + 2):
        if part < parts:
            for peer in range(part * per_part, (part + 1) * per_part):
                for step in range(per_peer):
                    page = order[peer * per_peer + step]
                    for kind, pool in enumerate((keys, values)):
                        pltpu.make_async_copy(
                            pool.at[page], buf.at[peer, kind, step], in_sems.at[part]
                        ).start()
        if part >= 2:
            mine = pl.ds((part - 2) * per_part, per_part)
            pltpu.make_async_copy(out.at[mine], buf.at[mine], in_sems.at[part - 2]).wait()
            pltpu.make_async_copy(buf.at[mine], out.at[mine], out_sems.at[part - 2]).start()
    for part in range(parts):
        mine = pl.ds(part * per_part, per_part)
        pltpu.make_async_copy(buf.at[mine], out.at[mine], out_sems.at[part]).wait()


def collect(order, keys, values, devices):
    pages, page_len, width = keys.shape
    shape = (devices, 2, pages // devices, page_len, width)
    parts = 16
    whole = pl.BlockSpec(memory_space=pl.ANY)
    return pl.pallas_call(
        collect_kernel,
        in_specs=[pl.BlockSpec(memory_space=pltpu.SMEM), whole, whole],
        out_specs=whole,
        out_shape=jax.ShapeDtypeStruct(shape, keys.dtype),
        scratch_shapes=[
            pltpu.VMEM(shape, keys.dtype),
            pltpu.SemaphoreType.DMA((parts,)),
            pltpu.SemaphoreType.DMA((parts,)),
        ],
        compiler_params=pltpu.CompilerParams(vmem_limit_bytes=VMEM_BYTES),
        cost_estimate=pl.CostEstimate(
            flops=0, bytes_accessed=8 * keys.size, transcendentals=0
        ),
        name="collect_pages",
    )(order, keys, values)


def place_kernel(
    placement, starts, fresh_keys, fresh_values, incoming, out_keys, out_values, buf, in_sems, out_sems
):
    slots, new_count, _ = fresh_keys.shape
    _, pages, page_len, _ = buf.shape
    per_slot = pages // slots

    def fetch(slot):
        for step in range(per_slot):
            page = slot * per_slot + step
            for kind in range(2):
                pltpu.make_async_copy(
                    incoming.at[placement[kind * pages + page]],
                    buf.at[kind, page],
                    in_sems.at[kind, slot],
                ).start()

    def finish(slot):
        mine = pl.ds(slot * per_slot, per_slot)
        for kind, (fresh, out) in enumerate(((fresh_keys, out_keys), (fresh_values, out_values))):
            pltpu.make_async_copy(out.at[mine], buf.at[kind, mine], in_sems.at[kind, slot]).wait()
            for token in range(new_count):
                spot = starts[slot] + token

                @pl.when((spot >= 0) & (spot < per_slot * page_len))
                def _():
                    page = slot * per_slot + spot // page_len
                    block = buf[kind, page].astype(jnp.float32)
                    here = lax.broadcasted_iota(jnp.int32, block.shape, 0) == spot % page_len
                    row = fresh[slot, pl.ds(token, 1), :]
                    buf[kind, page] = jnp.where(here, row, block).astype(buf.dtype)

            pltpu.make_async_copy(buf.at[kind, mine], out.at[mine], out_sems.at[kind, slot]).start()

    for slot in range(slots + 2):
        if slot < slots:
            fetch(slot)
        if slot >= 2:
            finish(slot - 2)
    for slot in range(slots):
        mine = pl.ds(slot * per_slot, per_slot)
        for kind, out in enumerate((out_keys, out_values)):
            pltpu.make_async_copy(buf.at[kind, mine], out.at[mine], out_sems.at[kind, slot]).wait()


def place(placement, starts, fresh_keys, fresh_values, incoming):
    slots = fresh_keys.shape[0]
    pages = incoming.shape[0] // 2
    shape = (pages,) + incoming.shape[1:]
    smem = pl.BlockSpec(memory_space=pltpu.SMEM)
    vmem = pl.BlockSpec(memory_space=pltpu.VMEM)
    whole = pl.BlockSpec(memory_space=pl.ANY)
    return pl.pallas_call(
        place_kernel,
        in_specs=[smem, smem, vmem, vmem, whole],
        out_specs=[whole, whole],
        out_shape=[jax.ShapeDtypeStruct(shape, incoming.dtype)] * 2,
        scratch_shapes=[
            pltpu.VMEM((2,) + shape, incoming.dtype),
            pltpu.SemaphoreType.DMA((2, slots)),
            pltpu.SemaphoreType.DMA((2, slots)),
        ],
        compiler_params=pltpu.CompilerParams(vmem_limit_bytes=VMEM_BYTES),
        cost_estimate=pl.CostEstimate(
            flops=0, bytes_accessed=4 * incoming.size, transcendentals=0
        ),
        name="place_pages",
    )(placement, starts, fresh_keys, fresh_values, incoming)


def push_kernel(sizes, spread, count, *refs):
    srcs, outs = refs[:count], refs[count : 2 * count]
    send_sems, recv_sems = refs[2 * count :]
    total = math.prod(sizes.values())
    me = 0
    for name, size in sizes.items():
        me = me * size + lax.axis_index(name)

    def coords(flat):
        found = {}
        for name, size in reversed(sizes.items()):
            found[name] = lax.rem(flat, size)
            flat = lax.div(flat, size)
        return found

    barrier = pltpu.get_barrier_semaphore()

    def greet(step, _):
        peer = lax.rem(me + step, total)
        pl.semaphore_signal(
            barrier, inc=1, device_id=coords(peer), device_id_type=pl.DeviceIdType.MESH
        )
        return 0

    lax.fori_loop(1, total, greet, 0)
    pl.semaphore_wait(barrier, total - 1)

    def copy(which, step, place):
        peer = lax.rem(me + step, total)
        src = srcs[which].at[peer] if spread else srcs[which]
        return pltpu.make_async_remote_copy(
            src_ref=src,
            dst_ref=outs[which].at[place],
            send_sem=send_sems.at[which, step],
            recv_sem=recv_sems.at[which, step],
            device_id=coords(peer),
            device_id_type=pl.DeviceIdType.MESH,
        )

    def send(step, _):
        for which in range(count):
            copy(which, step, me).start()
        return 0

    lax.fori_loop(1, total, send, 0)
    for which in range(count):
        outs[which][me] = srcs[which][me] if spread else srcs[which][...]

    def finish(step, _):
        for which in range(count):
            copy(which, step, lax.rem(me + total - step, total)).wait_recv()
            copy(which, step, me).wait_send()
        return 0

    lax.fori_loop(1, total, finish, 0)


def push(arrays, axes, spread, collective_id, name):
    sizes = {axis: lax.axis_size(axis) for axis in axes}
    total = math.prod(sizes.values())
    vmem = pl.BlockSpec(memory_space=pltpu.VMEM)
    shapes = [a.shape if spread else (total,) + a.shape for a in arrays]
    return pl.pallas_call(
        functools.partial(push_kernel, sizes, spread, len(arrays)),
        in_specs=[vmem] * len(arrays),
        out_specs=[vmem] * len(arrays),
        out_shape=[jax.ShapeDtypeStruct(s, a.dtype) for s, a in zip(shapes, arrays)],
        scratch_shapes=[
            pltpu.SemaphoreType.DMA((len(arrays), total)),
            pltpu.SemaphoreType.DMA((len(arrays), total)),
        ],
        compiler_params=pltpu.CompilerParams(
            collective_id=collective_id, has_side_effects=True, vmem_limit_bytes=VMEM_BYTES // 2
        ),
        name=name,
    )(*arrays)


def shards(
    new_tokens,
    norm_gain,
    w_query,
    w_key,
    w_value,
    w_out,
    pool_keys,
    pool_values,
    cache_lengths,
    owner,
    page_table,
):
    req_count = lax.axis_size("req")
    seq_count = lax.axis_size("seq")
    devices = req_count * seq_count
    req_index = lax.axis_index("req")
    seq_index = lax.axis_index("seq")
    device_index = req_index * seq_count + seq_index
    local_reqs, new_count, model_width = new_tokens.shape
    slot_total = owner.shape[0]
    pages_dev, page_len, kv_width = pool_keys.shape
    pages_req = page_table.shape[1]
    pages_home = pages_req // seq_count
    positions = pages_home * page_len
    per_peer = pages_dev // devices
    query_cols = w_query.shape[1]
    key_cols = w_key.shape[1]
    i32 = jnp.int32
    local_pages = jnp.arange(pages_dev, dtype=i32)

    logical = jnp.arange(pages_req, dtype=i32)[None, :]
    home_index = (
        (owner[:, None] // local_reqs * seq_count + logical // pages_home) * pages_dev
        + owner[:, None] % local_reqs * pages_home
        + logical % pages_home
    )
    held = page_table[None] == (device_index * pages_dev + local_pages)[:, None, None]
    held_homes = jnp.sum(jnp.where(held, home_index[None], 0), axis=(1, 2))
    send_rank = jnp.sum((held_homes[None, :] < held_homes[:, None]).astype(i32), axis=1)
    send_order = jnp.sum(
        jnp.where(send_rank[None, :] == local_pages[:, None], local_pages[None, :], 0), axis=1
    )

    outgoing = collect(send_order, pool_keys, pool_values, devices)
    slots = jnp.arange(slot_total, dtype=i32)
    slot_owned = owner[None, :] == slots[:, None]
    slot_request = jnp.sum(jnp.where(slot_owned, slots[None, :], 0), axis=1)
    slot_lengths = jnp.sum(jnp.where(slot_owned, cache_lengths[None, :], 0), axis=1)
    my_requests = lax.dynamic_slice_in_dim(slot_request, req_index * local_reqs, local_reqs)
    my_lengths = lax.dynamic_slice_in_dim(slot_lengths, req_index * local_reqs, local_reqs)
    seq_pages = lax.dynamic_slice_in_dim(page_table, seq_index * pages_home, pages_home, axis=1)
    is_mine = my_requests[:, None, None] == slots[None, :, None]
    source = jnp.sum(jnp.where(is_mine, seq_pages[None], 0), axis=1).reshape(-1) // pages_dev
    ahead = (source[None, :] == source[:, None]) & (local_pages[None, :] < local_pages[:, None])
    placement = source * (2 * per_peer) + jnp.sum(ahead.astype(i32), axis=1)
    placement = jnp.concatenate([placement, placement + per_peer])

    tokens_wide = new_tokens.astype(jnp.float32)
    square_mean = jnp.mean(tokens_wide * tokens_wide, axis=-1, keepdims=True)
    normed = (tokens_wide * lax.rsqrt(square_mean + NORM_EPS) * norm_gain).astype(jnp.bfloat16)
    normed = normed.reshape(local_reqs * new_count, model_width)
    flat_rows = push([normed], ("req",), False, 0, "gather_tokens")[0].reshape(-1, model_width)
    flat_rows, outgoing = lax.optimization_barrier((flat_rows, outgoing))
    incoming = lax.all_to_all(outgoing, ("req", "seq"), split_axis=0, concat_axis=0, tiled=True)
    incoming = incoming.reshape(2 * pages_dev, page_len, kv_width)
    new_index = jnp.arange(new_count, dtype=i32)
    places = slot_lengths[:, None] + new_index[None, :]
    heads = lambda w: jnp.dot(flat_rows, w, preferred_element_type=jnp.float32)
    queries_now = heads(w_query).reshape(slot_total, new_count, query_cols // HD, HD)
    keys_now = heads(w_key).reshape(slot_total, new_count, key_cols // HD, HD)
    queries_now = rotate(queries_now, places).reshape(slot_total * new_count, query_cols)
    keys_now = rotate(keys_now, places).reshape(slot_total * new_count, key_cols)
    projected = jnp.concatenate([queries_now, keys_now, heads(w_value)], axis=-1)
    every = push([projected.astype(jnp.bfloat16)], ("req",), False, 1, "gather_heads")[0]
    own_kv = key_cols // HD
    queries = every[..., :query_cols].reshape(
        req_count, slot_total, new_count, own_kv, GROUPS, HD
    )
    queries = jnp.transpose(queries, (0, 3, 1, 4, 2, 5)).reshape(KVH, -1, HD)

    def by_head(part):
        part = part.reshape(req_count, slot_total * new_count, own_kv, HD)
        return jnp.transpose(part, (0, 2, 1, 3)).reshape(KVH, slot_total * new_count, HD)

    def of_mine(part):
        part = part.reshape(req_count, slot_total, new_count, key_cols)
        part = lax.dynamic_slice_in_dim(part, req_index * local_reqs, local_reqs, axis=1)
        part = jnp.transpose(part, (1, 2, 0, 3)).reshape(local_reqs, new_count, kv_width)
        return part.astype(jnp.float32)

    new_keys = every[..., query_cols : query_cols + key_cols]
    new_values = every[..., query_cols + key_cols :]

    held_dev = held_homes // pages_dev
    held_slot = held_dev // seq_count * local_reqs + held_homes % pages_dev // pages_home
    held_first = (held_dev % seq_count * pages_home + held_homes % pages_home) * page_len
    held_length = jnp.sum(
        jnp.where(held_slot[:, None] == slots[None, :], slot_lengths[None, :], 0), axis=1
    )
    spots = held_first[:, None] + jnp.arange(page_len, dtype=i32)[None, :]
    page_info = jnp.where(spots < held_length[:, None], held_slot[:, None], -1).reshape(1, -1)
    own_info = jnp.where(device_index == 0, jnp.repeat(slots, new_count), -1).reshape(1, -1)
    total, peak, mass = attend(
        page_info,
        own_info,
        queries,
        pool_keys.reshape(pages_dev * page_len, kv_width),
        pool_values.reshape(pages_dev * page_len, kv_width),
        by_head(new_keys),
        by_head(new_values),
        new_count,
    )
    peak = peak[..., 0]
    mass = mass[..., 0]
    seq_slots = slot_total // seq_count
    part_rows = seq_slots * GROUPS * new_count

    def by_device(part):
        part = part.reshape((req_count, own_kv, seq_count, part_rows) + part.shape[2:])
        part = jnp.swapaxes(part, 1, 2)
        return part.reshape((devices, own_kv * part_rows) + part.shape[4:])

    stats = jnp.stack([by_device(peak), by_device(mass)], axis=1)
    stats = jnp.pad(stats, ((0, 0), (0, 6), (0, HD - own_kv * part_rows)))
    parts, stats = push(
        [by_device(total).astype(jnp.bfloat16), stats], ("req", "seq"), True, 2, "share_partials"
    )
    peaks = stats[:, 0, : own_kv * part_rows]
    rescale = jnp.exp(peaks - jnp.max(peaks, axis=0))
    mass = jnp.sum(stats[:, 1, : own_kv * part_rows] * rescale, axis=0)
    attended = jnp.sum(parts.astype(jnp.float32) * rescale[..., None], axis=0) / mass[:, None]
    attended = push([attended.astype(jnp.bfloat16)], ("seq",), False, 3, "gather_slots")[0]
    attended = attended.reshape(seq_count, own_kv, seq_slots, GROUPS, new_count, HD)
    attended = jnp.transpose(attended, (0, 2, 4, 1, 3, 5)).reshape(-1, query_cols)
    shares = jnp.dot(attended, w_out, preferred_element_type=jnp.float32).astype(jnp.bfloat16)
    shares = shares.reshape(req_count, local_reqs * new_count, model_width)
    shares = push([shares], ("req",), True, 4, "share_outputs")[0]
    summed = jnp.sum(shares.astype(jnp.float32), axis=0)
    out_hidden = (tokens_wide + summed.reshape(tokens_wide.shape)).astype(jnp.bfloat16)

    starts = my_lengths - seq_index * positions
    out_shape = (local_reqs, positions, kv_width)
    keys_out, values_out = place(
        placement, starts, of_mine(new_keys), of_mine(new_values), incoming
    )
    return (out_hidden, keys_out.reshape(out_shape), values_out.reshape(out_shape))


def solution(mesh):
    return jax.shard_map(
        shards,
        mesh=mesh,
        in_specs=(
            P("req", None, None),
            P(),
            P(None, "req"),
            P(None, "req"),
            P(None, "req"),
            P("req", None),
            P(("req", "seq"), None, None),
            P(("req", "seq"), None, None),
            P(),
            P(),
            P(),
        ),
        out_specs=(P("req", None, None), P("req", "seq", None), P("req", "seq", None)),
        check_vma=False,
    )
```

```python
import functools
import math

import jax
import jax.numpy as jnp
from jax import lax
from jax.experimental import pallas as pl
from jax.experimental.pallas import tpu as pltpu
from jax.sharding import PartitionSpec as P

H = 16
KVH = 8
HD = 128
GROUPS = H // KVH

NORM_EPS = 1e-05
ROPE_BASE = 1000000.0
MASKED = -1e30
VMEM_BYTES = 48 * 1024 * 1024


def rotate(values, places):
    half_dim = values.shape[-1] // 2
    steps_up = jnp.arange(half_dim, dtype=jnp.float32) * (2.0 / values.shape[-1])
    inverse = ROPE_BASE ** (-steps_up)
    angles = places.astype(jnp.float32)[..., None] * inverse
    cosine = jnp.cos(angles)[..., None, :]
    sine_part = jnp.sin(angles)[..., None, :]
    first_half = values[..., :half_dim]
    second_half = values[..., half_dim:]
    return jnp.concatenate(
        [
            first_half * cosine - second_half * sine_part,
            second_half * cosine + first_half * sine_part,
        ],
        axis=-1,
    )


def attend_kernel(
    new_count, page_info, own_info, q_ref, k_ref, v_ref, kn_ref, vn_ref, acc_ref, max_ref, sum_ref
):
    scale = 1.0 / math.sqrt(HD)
    q = q_ref[0]
    rows = q.shape[0]
    dims = (((1,), (1,)), ((), ()))
    scores = lax.dot_general(q, k_ref[...], dims, preferred_element_type=jnp.float32) * scale
    own = lax.dot_general(q, kn_ref[0], dims, preferred_element_type=jnp.float32) * scale
    row_ids = lax.broadcasted_iota(jnp.int32, (rows, 1), 0)
    row_slot = row_ids // (GROUPS * new_count)
    row_token = row_ids % new_count
    live = page_info[...] == row_slot
    own_token = lax.broadcasted_iota(jnp.int32, own.shape, 1) % new_count
    own_live = (own_info[...] == row_slot) & (own_token <= row_token)
    scores = jnp.where(live, scores, MASKED)
    own = jnp.where(own_live, own, MASKED)
    peak = jnp.maximum(
        jnp.max(scores, axis=-1, keepdims=True), jnp.max(own, axis=-1, keepdims=True)
    )
    weights = jnp.where(live, jnp.exp(scores - peak), 0.0)
    own_weights = jnp.where(own_live, jnp.exp(own - peak), 0.0)
    mass = jnp.sum(weights, axis=-1, keepdims=True) + jnp.sum(own_weights, axis=-1, keepdims=True)
    acc_ref[0] = jnp.dot(
        weights.astype(jnp.bfloat16), v_ref[...], preferred_element_type=jnp.float32
    ) + jnp.dot(own_weights.astype(jnp.bfloat16), vn_ref[0], preferred_element_type=jnp.float32)
    max_ref[0] = peak
    sum_ref[0] = mass


def attend(page_info, own_info, queries, keys, values, keys_new, values_new, new_count):
    rows = queries.shape[1]
    spots = keys.shape[0]
    own = keys_new.shape[1]
    whole = lambda shape: pl.BlockSpec(shape, lambda h: (0, 0))
    per_head = lambda shape: pl.BlockSpec((1,) + shape, lambda h: (h, 0, 0))
    return pl.pallas_call(
        functools.partial(attend_kernel, new_count),
        grid=(KVH,),
        in_specs=[
            whole((1, spots)),
            whole((1, own)),
            per_head((rows, HD)),
            pl.BlockSpec((spots, HD), lambda h: (0, h)),
            pl.BlockSpec((spots, HD), lambda h: (0, h)),
            per_head((own, HD)),
            per_head((own, HD)),
        ],
        out_specs=[per_head((rows, HD)), per_head((rows, 1)), per_head((rows, 1))],
        out_shape=[
            jax.ShapeDtypeStruct((KVH, rows, HD), jnp.float32),
            jax.ShapeDtypeStruct((KVH, rows, 1), jnp.float32),
            jax.ShapeDtypeStruct((KVH, rows, 1), jnp.float32),
        ],
        compiler_params=pltpu.CompilerParams(vmem_limit_bytes=VMEM_BYTES),
        cost_estimate=pl.CostEstimate(
            flops=4 * KVH * rows * spots * HD,
            bytes_accessed=4 * KVH * spots * HD,
            transcendentals=KVH * rows * spots,
        ),
        name="attend_held_pages",
    )(page_info, own_info, queries, keys, values, keys_new, values_new)


def collect_kernel(order, keys, values, out, buf, in_sems, out_sems):
    parts = in_sems.shape[0]
    devices, _, per_peer = buf.shape[:3]
    per_part = devices // parts
    for part in range(parts + 2):
        if part < parts:
            for peer in range(part * per_part, (part + 1) * per_part):
                for step in range(per_peer):
                    page = order[peer * per_peer + step]
                    for kind, pool in enumerate((keys, values)):
                        pltpu.make_async_copy(
                            pool.at[page], buf.at[peer, kind, step], in_sems.at[part]
                        ).start()
        if part >= 2:
            mine = pl.ds((part - 2) * per_part, per_part)
            pltpu.make_async_copy(out.at[mine], buf.at[mine], in_sems.at[part - 2]).wait()
            pltpu.make_async_copy(buf.at[mine], out.at[mine], out_sems.at[part - 2]).start()
    for part in range(parts):
        mine = pl.ds(part * per_part, per_part)
        pltpu.make_async_copy(buf.at[mine], out.at[mine], out_sems.at[part]).wait()


def collect(order, keys, values, devices):
    pages, page_len, width = keys.shape
    shape = (devices, 2, pages // devices, page_len, width)
    parts = 16
    whole = pl.BlockSpec(memory_space=pl.ANY)
    return pl.pallas_call(
        collect_kernel,
        in_specs=[pl.BlockSpec(memory_space=pltpu.SMEM), whole, whole],
        out_specs=whole,
        out_shape=jax.ShapeDtypeStruct(shape, keys.dtype),
        scratch_shapes=[
            pltpu.VMEM(shape, keys.dtype),
            pltpu.SemaphoreType.DMA((parts,)),
            pltpu.SemaphoreType.DMA((parts,)),
        ],
        compiler_params=pltpu.CompilerParams(vmem_limit_bytes=VMEM_BYTES),
        cost_estimate=pl.CostEstimate(
            flops=0, bytes_accessed=8 * keys.size, transcendentals=0
        ),
        name="collect_pages",
    )(order, keys, values)


def place_kernel(
    placement, starts, fresh_keys, fresh_values, incoming, out_keys, out_values, buf, in_sems, out_sems
):
    slots, new_count, _ = fresh_keys.shape
    _, pages, page_len, _ = buf.shape
    per_slot = pages // slots

    def fetch(slot):
        for step in range(per_slot):
            page = slot * per_slot + step
            for kind in range(2):
                pltpu.make_async_copy(
                    incoming.at[placement[kind * pages + page]],
                    buf.at[kind, page],
                    in_sems.at[kind, slot],
                ).start()

    def finish(slot):
        mine = pl.ds(slot * per_slot, per_slot)
        for kind, (fresh, out) in enumerate(((fresh_keys, out_keys), (fresh_values, out_values))):
            pltpu.make_async_copy(out.at[mine], buf.at[kind, mine], in_sems.at[kind, slot]).wait()
            for token in range(new_count):
                spot = starts[slot] + token

                @pl.when((spot >= 0) & (spot < per_slot * page_len))
                def _():
                    page = slot * per_slot + spot // page_len
                    block = buf[kind, page].astype(jnp.float32)
                    here = lax.broadcasted_iota(jnp.int32, block.shape, 0) == spot % page_len
                    row = fresh[slot, pl.ds(token, 1), :]
                    buf[kind, page] = jnp.where(here, row, block).astype(buf.dtype)

            pltpu.make_async_copy(buf.at[kind, mine], out.at[mine], out_sems.at[kind, slot]).start()

    for slot in range(slots + 2):
        if slot < slots:
            fetch(slot)
        if slot >= 2:
            finish(slot - 2)
    for slot in range(slots):
        mine = pl.ds(slot * per_slot, per_slot)
        for kind, out in enumerate((out_keys, out_values)):
            pltpu.make_async_copy(buf.at[kind, mine], out.at[mine], out_sems.at[kind, slot]).wait()


def place(placement, starts, fresh_keys, fresh_values, incoming):
    slots = fresh_keys.shape[0]
    pages = incoming.shape[0] // 2
    shape = (pages,) + incoming.shape[1:]
    smem = pl.BlockSpec(memory_space=pltpu.SMEM)
    vmem = pl.BlockSpec(memory_space=pltpu.VMEM)
    whole = pl.BlockSpec(memory_space=pl.ANY)
    return pl.pallas_call(
        place_kernel,
        in_specs=[smem, smem, vmem, vmem, whole],
        out_specs=[whole, whole],
        out_shape=[jax.ShapeDtypeStruct(shape, incoming.dtype)] * 2,
        scratch_shapes=[
            pltpu.VMEM((2,) + shape, incoming.dtype),
            pltpu.SemaphoreType.DMA((2, slots)),
            pltpu.SemaphoreType.DMA((2, slots)),
        ],
        compiler_params=pltpu.CompilerParams(vmem_limit_bytes=VMEM_BYTES),
        cost_estimate=pl.CostEstimate(
            flops=0, bytes_accessed=4 * incoming.size, transcendentals=0
        ),
        name="place_pages",
    )(placement, starts, fresh_keys, fresh_values, incoming)


def push_kernel(digits, spread, count, *refs):
    srcs, outs = refs[:count], refs[count : 2 * count]
    send_sems, recv_sems = refs[2 * count :]
    total = math.prod(size for _, _, size in digits)
    me = 0
    for name, stride, size in digits:
        me = me * size + lax.rem(lax.div(lax.axis_index(name), stride), size)

    def coords(flat):
        found = {}
        for name, stride, size in reversed(digits):
            index = found.get(name, lax.axis_index(name))
            mine = lax.rem(lax.div(lax.axis_index(name), stride), size)
            found[name] = index + (lax.rem(flat, size) - mine) * stride
            flat = lax.div(flat, size)
        return found

    barrier = pltpu.get_barrier_semaphore()

    def greet(step, _):
        peer = lax.rem(me + step, total)
        pl.semaphore_signal(
            barrier, inc=1, device_id=coords(peer), device_id_type=pl.DeviceIdType.MESH
        )
        return 0

    lax.fori_loop(1, total, greet, 0)
    pl.semaphore_wait(barrier, total - 1)

    def copy(which, step, place):
        peer = lax.rem(me + step, total)
        src = srcs[which].at[peer] if spread else srcs[which]
        return pltpu.make_async_remote_copy(
            src_ref=src,
            dst_ref=outs[which].at[place],
            send_sem=send_sems.at[which, step],
            recv_sem=recv_sems.at[which, step],
            device_id=coords(peer),
            device_id_type=pl.DeviceIdType.MESH,
        )

    def send(step, _):
        for which in range(count):
            copy(which, step, me).start()
        return 0

    lax.fori_loop(1, total, send, 0)
    for which in range(count):
        outs[which][me] = srcs[which][me] if spread else srcs[which][...]

    def finish(step, _):
        for which in range(count):
            copy(which, step, lax.rem(me + total - step, total)).wait_recv()
            copy(which, step, me).wait_send()
        return 0

    lax.fori_loop(1, total, finish, 0)


def push(arrays, digits, spread, collective_id, name):
    total = math.prod(size for _, _, size in digits)
    vmem = pl.BlockSpec(memory_space=pltpu.VMEM)
    shapes = [a.shape if spread else (total,) + a.shape for a in arrays]
    return pl.pallas_call(
        functools.partial(push_kernel, tuple(digits), spread, len(arrays)),
        in_specs=[vmem] * len(arrays),
        out_specs=[vmem] * len(arrays),
        out_shape=[jax.ShapeDtypeStruct(s, a.dtype) for s, a in zip(shapes, arrays)],
        scratch_shapes=[
            pltpu.SemaphoreType.DMA((len(arrays), total)),
            pltpu.SemaphoreType.DMA((len(arrays), total)),
        ],
        compiler_params=pltpu.CompilerParams(
            collective_id=collective_id, has_side_effects=True, vmem_limit_bytes=VMEM_BYTES // 2
        ),
        name=name,
    )(*arrays)


def shards(
    new_tokens,
    norm_gain,
    w_query,
    w_key,
    w_value,
    w_out,
    pool_keys,
    pool_values,
    cache_lengths,
    owner,
    page_table,
):
    req_count = lax.axis_size("req")
    seq_count = lax.axis_size("seq")
    devices = req_count * seq_count
    req_index = lax.axis_index("req")
    seq_index = lax.axis_index("seq")
    device_index = req_index * seq_count + seq_index
    local_reqs, new_count, model_width = new_tokens.shape
    slot_total = owner.shape[0]
    pages_dev, page_len, kv_width = pool_keys.shape
    pages_req = page_table.shape[1]
    pages_home = pages_req // seq_count
    positions = pages_home * page_len
    per_peer = pages_dev // devices
    query_cols = w_query.shape[1]
    key_cols = w_key.shape[1]
    low_count = 2 if seq_count % 2 == 0 else 1
    high_count = seq_count // low_count
    over_req = [("req", 1, req_count)]
    i32 = jnp.int32
    local_pages = jnp.arange(pages_dev, dtype=i32)

    logical = jnp.arange(pages_req, dtype=i32)[None, :]
    home_index = (
        (owner[:, None] // local_reqs * seq_count + logical // pages_home) * pages_dev
        + owner[:, None] % local_reqs * pages_home
        + logical % pages_home
    )
    held = page_table[None] == (device_index * pages_dev + local_pages)[:, None, None]
    held_homes = jnp.sum(jnp.where(held, home_index[None], 0), axis=(1, 2))
    send_rank = jnp.sum((held_homes[None, :] < held_homes[:, None]).astype(i32), axis=1)
    send_order = jnp.sum(
        jnp.where(send_rank[None, :] == local_pages[:, None], local_pages[None, :], 0), axis=1
    )

    outgoing = collect(send_order, pool_keys, pool_values, devices)
    slots = jnp.arange(slot_total, dtype=i32)
    slot_owned = owner[None, :] == slots[:, None]
    slot_request = jnp.sum(jnp.where(slot_owned, slots[None, :], 0), axis=1)
    slot_lengths = jnp.sum(jnp.where(slot_owned, cache_lengths[None, :], 0), axis=1)
    my_requests = lax.dynamic_slice_in_dim(slot_request, req_index * local_reqs, local_reqs)
    my_lengths = lax.dynamic_slice_in_dim(slot_lengths, req_index * local_reqs, local_reqs)
    seq_pages = lax.dynamic_slice_in_dim(page_table, seq_index * pages_home, pages_home, axis=1)
    is_mine = my_requests[:, None, None] == slots[None, :, None]
    source = jnp.sum(jnp.where(is_mine, seq_pages[None], 0), axis=1).reshape(-1) // pages_dev
    ahead = (source[None, :] == source[:, None]) & (local_pages[None, :] < local_pages[:, None])
    placement = source * (2 * per_peer) + jnp.sum(ahead.astype(i32), axis=1)
    placement = jnp.concatenate([placement, placement + per_peer])

    tokens_wide = new_tokens.astype(jnp.float32)
    square_mean = jnp.mean(tokens_wide * tokens_wide, axis=-1, keepdims=True)
    normed = (tokens_wide * lax.rsqrt(square_mean + NORM_EPS) * norm_gain).astype(jnp.bfloat16)
    normed = normed.reshape(local_reqs * new_count, model_width)
    normed, outgoing = lax.optimization_barrier((normed, outgoing))
    incoming = lax.all_to_all(outgoing, ("req", "seq"), split_axis=0, concat_axis=0, tiled=True)
    incoming = incoming.reshape(2 * pages_dev, page_len, kv_width)
    flat_rows = push([normed], over_req, False, 0, "gather_tokens")[0].reshape(-1, model_width)
    new_index = jnp.arange(new_count, dtype=i32)
    places = slot_lengths[:, None] + new_index[None, :]
    heads = lambda w: jnp.dot(flat_rows, w, preferred_element_type=jnp.float32)
    queries_now = heads(w_query).reshape(slot_total, new_count, query_cols // HD, HD)
    keys_now = heads(w_key).reshape(slot_total, new_count, key_cols // HD, HD)
    queries_now = rotate(queries_now, places).reshape(slot_total * new_count, query_cols)
    keys_now = rotate(keys_now, places).reshape(slot_total * new_count, key_cols)
    projected = jnp.concatenate([queries_now, keys_now, heads(w_value)], axis=-1)
    every = push([projected.astype(jnp.bfloat16)], over_req, False, 1, "gather_heads")[0]
    own_kv = key_cols // HD
    queries = every[..., :query_cols].reshape(
        req_count, slot_total, new_count, own_kv, GROUPS, HD
    )
    queries = jnp.transpose(queries, (0, 3, 1, 4, 2, 5)).reshape(KVH, -1, HD)

    def by_head(part):
        part = part.reshape(req_count, slot_total * new_count, own_kv, HD)
        return jnp.transpose(part, (0, 2, 1, 3)).reshape(KVH, slot_total * new_count, HD)

    def of_mine(part):
        part = part.reshape(req_count, slot_total, new_count, key_cols)
        part = lax.dynamic_slice_in_dim(part, req_index * local_reqs, local_reqs, axis=1)
        part = jnp.transpose(part, (1, 2, 0, 3)).reshape(local_reqs, new_count, kv_width)
        return part.astype(jnp.float32)

    new_keys = every[..., query_cols : query_cols + key_cols]
    new_values = every[..., query_cols + key_cols :]

    held_dev = held_homes // pages_dev
    held_slot = held_dev // seq_count * local_reqs + held_homes % pages_dev // pages_home
    held_first = (held_dev % seq_count * pages_home + held_homes % pages_home) * page_len
    held_length = jnp.sum(
        jnp.where(held_slot[:, None] == slots[None, :], slot_lengths[None, :], 0), axis=1
    )
    spots = held_first[:, None] + jnp.arange(page_len, dtype=i32)[None, :]
    page_info = jnp.where(spots < held_length[:, None], held_slot[:, None], -1).reshape(1, -1)
    own_info = jnp.where(device_index == 0, jnp.repeat(slots, new_count), -1).reshape(1, -1)
    total, peak, mass = attend(
        page_info,
        own_info,
        queries,
        pool_keys.reshape(pages_dev * page_len, kv_width),
        pool_values.reshape(pages_dev * page_len, kv_width),
        by_head(new_keys),
        by_head(new_values),
        new_count,
    )
    peak = peak[..., 0]
    mass = mass[..., 0]
    seq_slots = slot_total // seq_count
    part_rows = seq_slots * GROUPS * new_count

    def by_plane(part):
        part = part.reshape((req_count, own_kv, high_count, low_count, part_rows) + part.shape[2:])
        part = jnp.transpose(part, (0, 3, 2, 1, 4) + tuple(range(5, part.ndim)))
        return part.reshape((req_count * low_count, high_count * own_kv * part_rows) + part.shape[5:])

    def exchange(parts, peaks, masses, digits, collective_id, name):
        count = peaks.shape[1]
        stats = jnp.stack([peaks, masses], axis=1)
        stats = jnp.pad(stats, ((0, 0), (0, 6), (0, -count % HD)))
        parts, stats = push([parts.astype(jnp.bfloat16), stats], digits, True, collective_id, name)
        peaks = stats[:, 0, :count]
        top = jnp.max(peaks, axis=0)
        rescale = jnp.exp(peaks - top)
        masses = jnp.sum(stats[:, 1, :count] * rescale, axis=0)
        return jnp.sum(parts.astype(jnp.float32) * rescale[..., None], axis=0), top, masses

    plane = [("req", 1, req_count), ("seq", 1, low_count)]
    column = [("seq", low_count, high_count)]
    total, peak, mass = exchange(
        by_plane(total), by_plane(peak), by_plane(mass), plane, 2, "share_in_plane"
    )
    split = lambda part: part.reshape((high_count, own_kv * part_rows) + part.shape[1:])
    total, peak, mass = exchange(
        split(total), split(peak), split(mass), column, 5, "share_in_column"
    )
    attended = total / mass[:, None]
    over_seq = [("seq", 1, seq_count)]
    attended = push([attended.astype(jnp.bfloat16)], over_seq, False, 3, "gather_slots")[0]
    attended = attended.reshape(seq_count, own_kv, seq_slots, GROUPS, new_count, HD)
    attended = jnp.transpose(attended, (0, 2, 4, 1, 3, 5)).reshape(-1, query_cols)
    shares = jnp.dot(attended, w_out, preferred_element_type=jnp.float32).astype(jnp.bfloat16)
    shares = shares.reshape(req_count, local_reqs * new_count, model_width)
    shares = lax.all_to_all(shares, "req", split_axis=0, concat_axis=0, tiled=True)
    summed = jnp.sum(shares.astype(jnp.float32), axis=0)
    out_hidden = (tokens_wide + summed.reshape(tokens_wide.shape)).astype(jnp.bfloat16)

    starts = my_lengths - seq_index * positions
    out_shape = (local_reqs, positions, kv_width)
    keys_out, values_out = place(
        placement, starts, of_mine(new_keys), of_mine(new_values), incoming
    )
    return (out_hidden, keys_out.reshape(out_shape), values_out.reshape(out_shape))


def solution(mesh):
    return jax.shard_map(
        shards,
        mesh=mesh,
        in_specs=(
            P("req", None, None),
            P(),
            P(None, "req"),
            P(None, "req"),
            P(None, "req"),
            P("req", None),
            P(("req", "seq"), None, None),
            P(("req", "seq"), None, None),
            P(),
            P(),
            P(),
        ),
        out_specs=(P("req", None, None), P("req", "seq", None), P("req", "seq", None)),
        check_vma=False,
    )
```

```python
import functools
import math

import jax
import jax.numpy as jnp
from jax import lax
from jax.experimental import pallas as pl
from jax.experimental.pallas import tpu as pltpu
from jax.sharding import PartitionSpec as P

H = 16
KVH = 8
HD = 128
GROUPS = H // KVH

NORM_EPS = 1e-05
ROPE_BASE = 1000000.0
MASKED = -1e30
VMEM_BYTES = 48 * 1024 * 1024


def rotate(values, places):
    half_dim = values.shape[-1] // 2
    steps_up = jnp.arange(half_dim, dtype=jnp.float32) * (2.0 / values.shape[-1])
    inverse = ROPE_BASE ** (-steps_up)
    angles = places.astype(jnp.float32)[..., None] * inverse
    cosine = jnp.cos(angles)[..., None, :]
    sine_part = jnp.sin(angles)[..., None, :]
    first_half = values[..., :half_dim]
    second_half = values[..., half_dim:]
    return jnp.concatenate(
        [
            first_half * cosine - second_half * sine_part,
            second_half * cosine + first_half * sine_part,
        ],
        axis=-1,
    )


def attend_kernel(
    new_count, page_info, own_info, q_ref, k_ref, v_ref, kn_ref, vn_ref, acc_ref, max_ref, sum_ref
):
    scale = 1.0 / math.sqrt(HD)
    q = q_ref[0]
    rows = q.shape[0]
    dims = (((1,), (1,)), ((), ()))
    scores = lax.dot_general(q, k_ref[...], dims, preferred_element_type=jnp.float32) * scale
    own = lax.dot_general(q, kn_ref[0], dims, preferred_element_type=jnp.float32) * scale
    row_ids = lax.broadcasted_iota(jnp.int32, (rows, 1), 0)
    row_slot = row_ids // (GROUPS * new_count)
    row_token = row_ids % new_count
    live = page_info[...] == row_slot
    own_token = lax.broadcasted_iota(jnp.int32, own.shape, 1) % new_count
    own_live = (own_info[...] == row_slot) & (own_token <= row_token)
    scores = jnp.where(live, scores, MASKED)
    own = jnp.where(own_live, own, MASKED)
    peak = jnp.maximum(
        jnp.max(scores, axis=-1, keepdims=True), jnp.max(own, axis=-1, keepdims=True)
    )
    weights = jnp.where(live, jnp.exp(scores - peak), 0.0)
    own_weights = jnp.where(own_live, jnp.exp(own - peak), 0.0)
    mass = jnp.sum(weights, axis=-1, keepdims=True) + jnp.sum(own_weights, axis=-1, keepdims=True)
    acc_ref[0] = jnp.dot(
        weights.astype(jnp.bfloat16), v_ref[...], preferred_element_type=jnp.float32
    ) + jnp.dot(own_weights.astype(jnp.bfloat16), vn_ref[0], preferred_element_type=jnp.float32)
    max_ref[0] = peak
    sum_ref[0] = mass


def attend(page_info, own_info, queries, keys, values, keys_new, values_new, new_count):
    rows = queries.shape[1]
    spots = keys.shape[0]
    own = keys_new.shape[1]
    whole = lambda shape: pl.BlockSpec(shape, lambda h: (0, 0))
    per_head = lambda shape: pl.BlockSpec((1,) + shape, lambda h: (h, 0, 0))
    return pl.pallas_call(
        functools.partial(attend_kernel, new_count),
        grid=(KVH,),
        in_specs=[
            whole((1, spots)),
            whole((1, own)),
            per_head((rows, HD)),
            pl.BlockSpec((spots, HD), lambda h: (0, h)),
            pl.BlockSpec((spots, HD), lambda h: (0, h)),
            per_head((own, HD)),
            per_head((own, HD)),
        ],
        out_specs=[per_head((rows, HD)), per_head((rows, 1)), per_head((rows, 1))],
        out_shape=[
            jax.ShapeDtypeStruct((KVH, rows, HD), jnp.float32),
            jax.ShapeDtypeStruct((KVH, rows, 1), jnp.float32),
            jax.ShapeDtypeStruct((KVH, rows, 1), jnp.float32),
        ],
        compiler_params=pltpu.CompilerParams(vmem_limit_bytes=VMEM_BYTES),
        cost_estimate=pl.CostEstimate(
            flops=4 * KVH * rows * spots * HD,
            bytes_accessed=4 * KVH * spots * HD,
            transcendentals=KVH * rows * spots,
        ),
        name="attend_held_pages",
    )(page_info, own_info, queries, keys, values, keys_new, values_new)


def collect_kernel(order, keys, values, out, buf, in_sems, out_sems):
    parts = in_sems.shape[0]
    devices, _, per_peer = buf.shape[:3]
    per_part = devices // parts
    for part in range(parts + 2):
        if part < parts:
            for peer in range(part * per_part, (part + 1) * per_part):
                for step in range(per_peer):
                    page = order[peer * per_peer + step]
                    for kind, pool in enumerate((keys, values)):
                        pltpu.make_async_copy(
                            pool.at[page], buf.at[peer, kind, step], in_sems.at[part]
                        ).start()
        if part >= 2:
            mine = pl.ds((part - 2) * per_part, per_part)
            pltpu.make_async_copy(out.at[mine], buf.at[mine], in_sems.at[part - 2]).wait()
            pltpu.make_async_copy(buf.at[mine], out.at[mine], out_sems.at[part - 2]).start()
    for part in range(parts):
        mine = pl.ds(part * per_part, per_part)
        pltpu.make_async_copy(buf.at[mine], out.at[mine], out_sems.at[part]).wait()


def collect(order, keys, values, devices):
    pages, page_len, width = keys.shape
    shape = (devices, 2, pages // devices, page_len, width)
    parts = 16
    whole = pl.BlockSpec(memory_space=pl.ANY)
    return pl.pallas_call(
        collect_kernel,
        in_specs=[pl.BlockSpec(memory_space=pltpu.SMEM), whole, whole],
        out_specs=whole,
        out_shape=jax.ShapeDtypeStruct(shape, keys.dtype),
        scratch_shapes=[
            pltpu.VMEM(shape, keys.dtype),
            pltpu.SemaphoreType.DMA((parts,)),
            pltpu.SemaphoreType.DMA((parts,)),
        ],
        compiler_params=pltpu.CompilerParams(vmem_limit_bytes=VMEM_BYTES),
        cost_estimate=pl.CostEstimate(
            flops=0, bytes_accessed=8 * keys.size, transcendentals=0
        ),
        name="collect_pages",
    )(order, keys, values)


def place_kernel(
    placement, starts, fresh_keys, fresh_values, incoming, out_keys, out_values, buf, in_sems, out_sems
):
    slots, new_count, _ = fresh_keys.shape
    _, pages, page_len, _ = buf.shape
    per_slot = pages // slots

    def fetch(slot):
        for step in range(per_slot):
            page = slot * per_slot + step
            for kind in range(2):
                pltpu.make_async_copy(
                    incoming.at[placement[kind * pages + page]],
                    buf.at[kind, page],
                    in_sems.at[kind, slot],
                ).start()

    def finish(slot):
        mine = pl.ds(slot * per_slot, per_slot)
        for kind, (fresh, out) in enumerate(((fresh_keys, out_keys), (fresh_values, out_values))):
            pltpu.make_async_copy(out.at[mine], buf.at[kind, mine], in_sems.at[kind, slot]).wait()
            for token in range(new_count):
                spot = starts[slot] + token

                @pl.when((spot >= 0) & (spot < per_slot * page_len))
                def _():
                    page = slot * per_slot + spot // page_len
                    block = buf[kind, page].astype(jnp.float32)
                    here = lax.broadcasted_iota(jnp.int32, block.shape, 0) == spot % page_len
                    row = fresh[slot, pl.ds(token, 1), :]
                    buf[kind, page] = jnp.where(here, row, block).astype(buf.dtype)

            pltpu.make_async_copy(buf.at[kind, mine], out.at[mine], out_sems.at[kind, slot]).start()

    for slot in range(slots + 2):
        if slot < slots:
            fetch(slot)
        if slot >= 2:
            finish(slot - 2)
    for slot in range(slots):
        mine = pl.ds(slot * per_slot, per_slot)
        for kind, out in enumerate((out_keys, out_values)):
            pltpu.make_async_copy(buf.at[kind, mine], out.at[mine], out_sems.at[kind, slot]).wait()


def place(placement, starts, fresh_keys, fresh_values, incoming):
    slots = fresh_keys.shape[0]
    pages = incoming.shape[0] // 2
    shape = (pages,) + incoming.shape[1:]
    smem = pl.BlockSpec(memory_space=pltpu.SMEM)
    vmem = pl.BlockSpec(memory_space=pltpu.VMEM)
    whole = pl.BlockSpec(memory_space=pl.ANY)
    return pl.pallas_call(
        place_kernel,
        in_specs=[smem, smem, vmem, vmem, whole],
        out_specs=[whole, whole],
        out_shape=[jax.ShapeDtypeStruct(shape, incoming.dtype)] * 2,
        scratch_shapes=[
            pltpu.VMEM((2,) + shape, incoming.dtype),
            pltpu.SemaphoreType.DMA((2, slots)),
            pltpu.SemaphoreType.DMA((2, slots)),
        ],
        compiler_params=pltpu.CompilerParams(vmem_limit_bytes=VMEM_BYTES),
        cost_estimate=pl.CostEstimate(
            flops=0, bytes_accessed=4 * incoming.size, transcendentals=0
        ),
        name="place_pages",
    )(placement, starts, fresh_keys, fresh_values, incoming)


def push_kernel(digits, spread, count, *refs):
    srcs, outs = refs[:count], refs[count : 2 * count]
    send_sems, recv_sems = refs[2 * count :]
    total = math.prod(size for _, _, size in digits)
    me = 0
    for name, stride, size in digits:
        me = me * size + lax.rem(lax.div(lax.axis_index(name), stride), size)

    def coords(flat):
        found = {}
        for name, stride, size in reversed(digits):
            index = found.get(name, lax.axis_index(name))
            mine = lax.rem(lax.div(lax.axis_index(name), stride), size)
            found[name] = index + (lax.rem(flat, size) - mine) * stride
            flat = lax.div(flat, size)
        return found

    barrier = pltpu.get_barrier_semaphore()

    def greet(step, _):
        peer = lax.rem(me + step, total)
        pl.semaphore_signal(
            barrier, inc=1, device_id=coords(peer), device_id_type=pl.DeviceIdType.MESH
        )
        return 0

    lax.fori_loop(1, total, greet, 0)
    pl.semaphore_wait(barrier, total - 1)

    def copy(which, step, place):
        peer = lax.rem(me + step, total)
        src = srcs[which].at[peer] if spread else srcs[which]
        return pltpu.make_async_remote_copy(
            src_ref=src,
            dst_ref=outs[which].at[place],
            send_sem=send_sems.at[which, step],
            recv_sem=recv_sems.at[which, step],
            device_id=coords(peer),
            device_id_type=pl.DeviceIdType.MESH,
        )

    def send(step, _):
        for which in range(count):
            copy(which, step, me).start()
        return 0

    lax.fori_loop(1, total, send, 0)
    for which in range(count):
        outs[which][me] = srcs[which][me] if spread else srcs[which][...]

    def finish(step, _):
        for which in range(count):
            copy(which, step, lax.rem(me + total - step, total)).wait_recv()
            copy(which, step, me).wait_send()
        return 0

    lax.fori_loop(1, total, finish, 0)


def push(arrays, digits, spread, collective_id, name):
    total = math.prod(size for _, _, size in digits)
    vmem = pl.BlockSpec(memory_space=pltpu.VMEM)
    shapes = [a.shape if spread else (total,) + a.shape for a in arrays]
    return pl.pallas_call(
        functools.partial(push_kernel, tuple(digits), spread, len(arrays)),
        in_specs=[vmem] * len(arrays),
        out_specs=[vmem] * len(arrays),
        out_shape=[jax.ShapeDtypeStruct(s, a.dtype) for s, a in zip(shapes, arrays)],
        scratch_shapes=[
            pltpu.SemaphoreType.DMA((len(arrays), total)),
            pltpu.SemaphoreType.DMA((len(arrays), total)),
        ],
        compiler_params=pltpu.CompilerParams(
            collective_id=collective_id, has_side_effects=True, vmem_limit_bytes=VMEM_BYTES // 2
        ),
        name=name,
    )(*arrays)


def shards(
    new_tokens,
    norm_gain,
    w_query,
    w_key,
    w_value,
    w_out,
    pool_keys,
    pool_values,
    cache_lengths,
    owner,
    page_table,
):
    req_count = lax.axis_size("req")
    seq_count = lax.axis_size("seq")
    devices = req_count * seq_count
    req_index = lax.axis_index("req")
    seq_index = lax.axis_index("seq")
    device_index = req_index * seq_count + seq_index
    local_reqs, new_count, model_width = new_tokens.shape
    slot_total = owner.shape[0]
    pages_dev, page_len, kv_width = pool_keys.shape
    pages_req = page_table.shape[1]
    pages_home = pages_req // seq_count
    positions = pages_home * page_len
    per_peer = pages_dev // devices
    query_cols = w_query.shape[1]
    key_cols = w_key.shape[1]
    low_count = 2 if seq_count % 2 == 0 else 1
    high_count = seq_count // low_count
    over_req = [("req", 1, req_count)]
    i32 = jnp.int32
    local_pages = jnp.arange(pages_dev, dtype=i32)

    logical = jnp.arange(pages_req, dtype=i32)[None, :]
    home_index = (
        (owner[:, None] // local_reqs * seq_count + logical // pages_home) * pages_dev
        + owner[:, None] % local_reqs * pages_home
        + logical % pages_home
    )
    held = page_table[None] == (device_index * pages_dev + local_pages)[:, None, None]
    held_homes = jnp.sum(jnp.where(held, home_index[None], 0), axis=(1, 2))
    send_rank = jnp.sum((held_homes[None, :] < held_homes[:, None]).astype(i32), axis=1)
    send_order = jnp.sum(
        jnp.where(send_rank[None, :] == local_pages[:, None], local_pages[None, :], 0), axis=1
    )

    outgoing = collect(send_order, pool_keys, pool_values, devices)
    slots = jnp.arange(slot_total, dtype=i32)
    slot_owned = owner[None, :] == slots[:, None]
    slot_request = jnp.sum(jnp.where(slot_owned, slots[None, :], 0), axis=1)
    slot_lengths = jnp.sum(jnp.where(slot_owned, cache_lengths[None, :], 0), axis=1)
    my_requests = lax.dynamic_slice_in_dim(slot_request, req_index * local_reqs, local_reqs)
    my_lengths = lax.dynamic_slice_in_dim(slot_lengths, req_index * local_reqs, local_reqs)
    seq_pages = lax.dynamic_slice_in_dim(page_table, seq_index * pages_home, pages_home, axis=1)
    is_mine = my_requests[:, None, None] == slots[None, :, None]
    source = jnp.sum(jnp.where(is_mine, seq_pages[None], 0), axis=1).reshape(-1) // pages_dev
    ahead = (source[None, :] == source[:, None]) & (local_pages[None, :] < local_pages[:, None])
    placement = source * (2 * per_peer) + jnp.sum(ahead.astype(i32), axis=1)
    placement = jnp.concatenate([placement, placement + per_peer])

    tokens_wide = new_tokens.astype(jnp.float32)
    square_mean = jnp.mean(tokens_wide * tokens_wide, axis=-1, keepdims=True)
    normed = (tokens_wide * lax.rsqrt(square_mean + NORM_EPS) * norm_gain).astype(jnp.bfloat16)
    normed = normed.reshape(local_reqs * new_count, model_width)
    normed, outgoing = lax.optimization_barrier((normed, outgoing))
    incoming = lax.all_to_all(outgoing, ("req", "seq"), split_axis=0, concat_axis=0, tiled=True)
    incoming = incoming.reshape(2 * pages_dev, page_len, kv_width)
    flat_rows = push([normed], over_req, False, 0, "gather_tokens")[0].reshape(-1, model_width)
    new_index = jnp.arange(new_count, dtype=i32)
    places = slot_lengths[:, None] + new_index[None, :]
    heads = lambda w: jnp.dot(flat_rows, w, preferred_element_type=jnp.float32)
    queries_now = heads(w_query).reshape(slot_total, new_count, query_cols // HD, HD)
    keys_now = heads(w_key).reshape(slot_total, new_count, key_cols // HD, HD)
    queries_now = rotate(queries_now, places).reshape(slot_total * new_count, query_cols)
    keys_now = rotate(keys_now, places).reshape(slot_total * new_count, key_cols)
    projected = jnp.concatenate([queries_now, keys_now, heads(w_value)], axis=-1)
    every = push([projected.astype(jnp.bfloat16)], over_req, False, 1, "gather_heads")[0]
    own_kv = key_cols // HD
    queries = every[..., :query_cols].reshape(
        req_count, slot_total, new_count, own_kv, GROUPS, HD
    )
    queries = jnp.transpose(queries, (0, 3, 1, 4, 2, 5)).reshape(KVH, -1, HD)

    def by_head(part):
        part = part.reshape(req_count, slot_total * new_count, own_kv, HD)
        return jnp.transpose(part, (0, 2, 1, 3)).reshape(KVH, slot_total * new_count, HD)

    def of_mine(part):
        part = part.reshape(req_count, slot_total, new_count, key_cols)
        part = lax.dynamic_slice_in_dim(part, req_index * local_reqs, local_reqs, axis=1)
        part = jnp.transpose(part, (1, 2, 0, 3)).reshape(local_reqs, new_count, kv_width)
        return part.astype(jnp.float32)

    new_keys = every[..., query_cols : query_cols + key_cols]
    new_values = every[..., query_cols + key_cols :]

    held_dev = held_homes // pages_dev
    held_slot = held_dev // seq_count * local_reqs + held_homes % pages_dev // pages_home
    held_first = (held_dev % seq_count * pages_home + held_homes % pages_home) * page_len
    held_length = jnp.sum(
        jnp.where(held_slot[:, None] == slots[None, :], slot_lengths[None, :], 0), axis=1
    )
    spots = held_first[:, None] + jnp.arange(page_len, dtype=i32)[None, :]
    page_info = jnp.where(spots < held_length[:, None], held_slot[:, None], -1).reshape(1, -1)
    own_info = jnp.where(device_index == 0, jnp.repeat(slots, new_count), -1).reshape(1, -1)
    total, peak, mass = attend(
        page_info,
        own_info,
        queries,
        pool_keys.reshape(pages_dev * page_len, kv_width),
        pool_values.reshape(pages_dev * page_len, kv_width),
        by_head(new_keys),
        by_head(new_values),
        new_count,
    )
    peak = peak[..., 0]
    mass = mass[..., 0]
    seq_slots = slot_total // seq_count
    part_rows = seq_slots * GROUPS * new_count

    def by_plane(part):
        part = part.reshape((req_count, own_kv, high_count, low_count, part_rows) + part.shape[2:])
        part = jnp.transpose(part, (0, 3, 2, 1, 4) + tuple(range(5, part.ndim)))
        return part.reshape((req_count * low_count, high_count * own_kv * part_rows) + part.shape[5:])

    def exchange(parts, peaks, masses, digits, spread, collective_id, name):
        count = peaks.shape[-1]
        stats = jnp.stack([peaks, masses], axis=-2)
        wide = ((0, 0),) * (stats.ndim - 2)
        stats = jnp.pad(stats, wide + ((0, 6), (0, -count % HD)))
        parts, stats = push([parts.astype(jnp.bfloat16), stats], digits, spread, collective_id, name)
        peaks = stats[:, 0, :count]
        top = jnp.max(peaks, axis=0)
        rescale = jnp.exp(peaks - top)
        masses = jnp.sum(stats[:, 1, :count] * rescale, axis=0)
        return jnp.sum(parts.astype(jnp.float32) * rescale[..., None], axis=0), top, masses

    plane = [("req", 1, req_count), ("seq", 1, low_count)]
    column = [("seq", low_count, high_count)]
    total, peak, mass = exchange(
        by_plane(total), by_plane(peak), by_plane(mass), plane, True, 2, "share_in_plane"
    )
    total, peak, mass = exchange(total, peak, mass, column, False, 5, "share_in_column")
    attended = (total / mass[:, None]).astype(jnp.bfloat16)
    attended = attended.reshape(high_count, own_kv, seq_slots, GROUPS, new_count, HD)
    attended = jnp.transpose(attended, (0, 2, 4, 1, 3, 5)).reshape(-1, query_cols)
    shares = jnp.dot(attended, w_out, preferred_element_type=jnp.float32).astype(jnp.bfloat16)
    shares = shares.reshape(req_count, 1, -1, model_width)
    shares = jnp.broadcast_to(shares, (req_count, low_count) + shares.shape[2:])
    shares = shares.reshape((req_count * low_count,) + shares.shape[2:])
    shares = push([shares], plane, True, 4, "share_outputs")[0]
    shares = shares.reshape(
        req_count, low_count, high_count // req_count, seq_slots * new_count, model_width
    )
    summed = jnp.swapaxes(jnp.sum(shares.astype(jnp.float32), axis=0), 0, 1)
    out_hidden = (tokens_wide + summed.reshape(tokens_wide.shape)).astype(jnp.bfloat16)

    starts = my_lengths - seq_index * positions
    out_shape = (local_reqs, positions, kv_width)
    keys_out, values_out = place(
        placement, starts, of_mine(new_keys), of_mine(new_values), incoming
    )
    return (out_hidden, keys_out.reshape(out_shape), values_out.reshape(out_shape))


def solution(mesh):
    return jax.shard_map(
        shards,
        mesh=mesh,
        in_specs=(
            P("req", None, None),
            P(),
            P(None, "req"),
            P(None, "req"),
            P(None, "req"),
            P("req", None),
            P(("req", "seq"), None, None),
            P(("req", "seq"), None, None),
            P(),
            P(),
            P(),
        ),
        out_specs=(P("req", None, None), P("req", "seq", None), P("req", "seq", None)),
        check_vma=False,
    )
```

```python
import functools
import math

import jax
import jax.numpy as jnp
from jax import lax
from jax.experimental import pallas as pl
from jax.experimental.pallas import tpu as pltpu
from jax.sharding import PartitionSpec as P

H = 16
KVH = 8
HD = 128
GROUPS = H // KVH

NORM_EPS = 1e-05
ROPE_BASE = 1000000.0
MASKED = -1e30
VMEM_BYTES = 48 * 1024 * 1024


def rotate(values, places):
    half_dim = values.shape[-1] // 2
    steps_up = jnp.arange(half_dim, dtype=jnp.float32) * (2.0 / values.shape[-1])
    inverse = ROPE_BASE ** (-steps_up)
    angles = places.astype(jnp.float32)[..., None] * inverse
    cosine = jnp.cos(angles)[..., None, :]
    sine_part = jnp.sin(angles)[..., None, :]
    first_half = values[..., :half_dim]
    second_half = values[..., half_dim:]
    return jnp.concatenate(
        [
            first_half * cosine - second_half * sine_part,
            second_half * cosine + first_half * sine_part,
        ],
        axis=-1,
    )


def attend_kernel(
    new_count, page_info, own_info, q_ref, k_ref, v_ref, kn_ref, vn_ref, acc_ref, max_ref, sum_ref
):
    scale = 1.0 / math.sqrt(HD)
    q = q_ref[0]
    rows = q.shape[0]
    dims = (((1,), (1,)), ((), ()))
    scores = lax.dot_general(q, k_ref[...], dims, preferred_element_type=jnp.float32) * scale
    own = lax.dot_general(q, kn_ref[0], dims, preferred_element_type=jnp.float32) * scale
    row_ids = lax.broadcasted_iota(jnp.int32, (rows, 1), 0)
    row_slot = row_ids // (GROUPS * new_count)
    row_token = row_ids % new_count
    live = page_info[...] == row_slot
    own_token = lax.broadcasted_iota(jnp.int32, own.shape, 1) % new_count
    own_live = (own_info[...] == row_slot) & (own_token <= row_token)
    scores = jnp.where(live, scores, MASKED)
    own = jnp.where(own_live, own, MASKED)
    peak = jnp.maximum(
        jnp.max(scores, axis=-1, keepdims=True), jnp.max(own, axis=-1, keepdims=True)
    )
    weights = jnp.where(live, jnp.exp(scores - peak), 0.0)
    own_weights = jnp.where(own_live, jnp.exp(own - peak), 0.0)
    mass = jnp.sum(weights, axis=-1, keepdims=True) + jnp.sum(own_weights, axis=-1, keepdims=True)
    acc_ref[0] = jnp.dot(
        weights.astype(jnp.bfloat16), v_ref[...], preferred_element_type=jnp.float32
    ) + jnp.dot(own_weights.astype(jnp.bfloat16), vn_ref[0], preferred_element_type=jnp.float32)
    max_ref[0] = peak
    sum_ref[0] = mass


def attend(page_info, own_info, queries, keys, values, keys_new, values_new, new_count):
    rows = queries.shape[1]
    spots = keys.shape[0]
    own = keys_new.shape[1]
    whole = lambda shape: pl.BlockSpec(shape, lambda h: (0, 0))
    per_head = lambda shape: pl.BlockSpec((1,) + shape, lambda h: (h, 0, 0))
    return pl.pallas_call(
        functools.partial(attend_kernel, new_count),
        grid=(KVH,),
        in_specs=[
            whole((1, spots)),
            whole((1, own)),
            per_head((rows, HD)),
            pl.BlockSpec((spots, HD), lambda h: (0, h)),
            pl.BlockSpec((spots, HD), lambda h: (0, h)),
            per_head((own, HD)),
            per_head((own, HD)),
        ],
        out_specs=[per_head((rows, HD)), per_head((rows, 1)), per_head((rows, 1))],
        out_shape=[
            jax.ShapeDtypeStruct((KVH, rows, HD), jnp.float32),
            jax.ShapeDtypeStruct((KVH, rows, 1), jnp.float32),
            jax.ShapeDtypeStruct((KVH, rows, 1), jnp.float32),
        ],
        compiler_params=pltpu.CompilerParams(vmem_limit_bytes=VMEM_BYTES),
        cost_estimate=pl.CostEstimate(
            flops=4 * KVH * rows * spots * HD,
            bytes_accessed=4 * KVH * spots * HD,
            transcendentals=KVH * rows * spots,
        ),
        name="attend_held_pages",
    )(page_info, own_info, queries, keys, values, keys_new, values_new)


def collect_kernel(order, keys, values, out, buf, in_sems, out_sems):
    parts = in_sems.shape[0]
    devices, _, per_peer = buf.shape[:3]
    per_part = devices // parts
    for part in range(parts + 2):
        if part < parts:
            for peer in range(part * per_part, (part + 1) * per_part):
                for step in range(per_peer):
                    page = order[peer * per_peer + step]
                    for kind, pool in enumerate((keys, values)):
                        pltpu.make_async_copy(
                            pool.at[page], buf.at[peer, kind, step], in_sems.at[part]
                        ).start()
        if part >= 2:
            mine = pl.ds((part - 2) * per_part, per_part)
            pltpu.make_async_copy(out.at[mine], buf.at[mine], in_sems.at[part - 2]).wait()
            pltpu.make_async_copy(buf.at[mine], out.at[mine], out_sems.at[part - 2]).start()
    for part in range(parts):
        mine = pl.ds(part * per_part, per_part)
        pltpu.make_async_copy(buf.at[mine], out.at[mine], out_sems.at[part]).wait()


def collect(order, keys, values, devices):
    pages, page_len, width = keys.shape
    shape = (devices, 2, pages // devices, page_len, width)
    parts = 16
    whole = pl.BlockSpec(memory_space=pl.ANY)
    return pl.pallas_call(
        collect_kernel,
        in_specs=[pl.BlockSpec(memory_space=pltpu.SMEM), whole, whole],
        out_specs=whole,
        out_shape=jax.ShapeDtypeStruct(shape, keys.dtype),
        scratch_shapes=[
            pltpu.VMEM(shape, keys.dtype),
            pltpu.SemaphoreType.DMA((parts,)),
            pltpu.SemaphoreType.DMA((parts,)),
        ],
        compiler_params=pltpu.CompilerParams(vmem_limit_bytes=VMEM_BYTES),
        cost_estimate=pl.CostEstimate(
            flops=0, bytes_accessed=8 * keys.size, transcendentals=0
        ),
        name="collect_pages",
    )(order, keys, values)


def place_kernel(
    placement, starts, fresh_keys, fresh_values, incoming, out_keys, out_values, buf, in_sems, out_sems
):
    slots, new_count, _ = fresh_keys.shape
    _, pages, page_len, _ = buf.shape
    per_slot = pages // slots

    def fetch(slot):
        for step in range(per_slot):
            page = slot * per_slot + step
            for kind in range(2):
                pltpu.make_async_copy(
                    incoming.at[placement[kind * pages + page]],
                    buf.at[kind, page],
                    in_sems.at[kind, slot],
                ).start()

    def finish(slot):
        mine = pl.ds(slot * per_slot, per_slot)
        for kind, (fresh, out) in enumerate(((fresh_keys, out_keys), (fresh_values, out_values))):
            pltpu.make_async_copy(out.at[mine], buf.at[kind, mine], in_sems.at[kind, slot]).wait()
            for token in range(new_count):
                spot = starts[slot] + token

                @pl.when((spot >= 0) & (spot < per_slot * page_len))
                def _():
                    page = slot * per_slot + spot // page_len
                    block = buf[kind, page].astype(jnp.float32)
                    here = lax.broadcasted_iota(jnp.int32, block.shape, 0) == spot % page_len
                    row = fresh[slot, pl.ds(token, 1), :]
                    buf[kind, page] = jnp.where(here, row, block).astype(buf.dtype)

            pltpu.make_async_copy(buf.at[kind, mine], out.at[mine], out_sems.at[kind, slot]).start()

    for slot in range(slots + 2):
        if slot < slots:
            fetch(slot)
        if slot >= 2:
            finish(slot - 2)
    for slot in range(slots):
        mine = pl.ds(slot * per_slot, per_slot)
        for kind, out in enumerate((out_keys, out_values)):
            pltpu.make_async_copy(buf.at[kind, mine], out.at[mine], out_sems.at[kind, slot]).wait()


def place(placement, starts, fresh_keys, fresh_values, incoming):
    slots = fresh_keys.shape[0]
    pages = incoming.shape[0] // 2
    shape = (pages,) + incoming.shape[1:]
    smem = pl.BlockSpec(memory_space=pltpu.SMEM)
    vmem = pl.BlockSpec(memory_space=pltpu.VMEM)
    whole = pl.BlockSpec(memory_space=pl.ANY)
    return pl.pallas_call(
        place_kernel,
        in_specs=[smem, smem, vmem, vmem, whole],
        out_specs=[whole, whole],
        out_shape=[jax.ShapeDtypeStruct(shape, incoming.dtype)] * 2,
        scratch_shapes=[
            pltpu.VMEM((2,) + shape, incoming.dtype),
            pltpu.SemaphoreType.DMA((2, slots)),
            pltpu.SemaphoreType.DMA((2, slots)),
        ],
        compiler_params=pltpu.CompilerParams(vmem_limit_bytes=VMEM_BYTES),
        cost_estimate=pl.CostEstimate(
            flops=0, bytes_accessed=4 * incoming.size, transcendentals=0
        ),
        name="place_pages",
    )(placement, starts, fresh_keys, fresh_values, incoming)


def push_kernel(digits, spread, count, *refs):
    srcs, outs = refs[:count], refs[count : 2 * count]
    send_sems, recv_sems = refs[2 * count :]
    total = math.prod(size for _, _, size in digits)
    me = 0
    for name, stride, size in digits:
        me = me * size + lax.rem(lax.div(lax.axis_index(name), stride), size)

    def coords(flat):
        found = {}
        for name, stride, size in reversed(digits):
            index = found.get(name, lax.axis_index(name))
            mine = lax.rem(lax.div(lax.axis_index(name), stride), size)
            found[name] = index + (lax.rem(flat, size) - mine) * stride
            flat = lax.div(flat, size)
        return found

    barrier = pltpu.get_barrier_semaphore()

    def greet(step, _):
        peer = lax.rem(me + step, total)
        pl.semaphore_signal(
            barrier, inc=1, device_id=coords(peer), device_id_type=pl.DeviceIdType.MESH
        )
        return 0

    lax.fori_loop(1, total, greet, 0)
    pl.semaphore_wait(barrier, total - 1)

    def copy(which, step, place):
        peer = lax.rem(me + step, total)
        src = srcs[which].at[peer] if spread else srcs[which]
        return pltpu.make_async_remote_copy(
            src_ref=src,
            dst_ref=outs[which].at[place],
            send_sem=send_sems.at[which, step],
            recv_sem=recv_sems.at[which, step],
            device_id=coords(peer),
            device_id_type=pl.DeviceIdType.MESH,
        )

    def send(step, _):
        for which in range(count):
            copy(which, step, me).start()
        return 0

    lax.fori_loop(1, total, send, 0)
    for which in range(count):
        outs[which][me] = srcs[which][me] if spread else srcs[which][...]

    def finish(step, _):
        for which in range(count):
            copy(which, step, lax.rem(me + total - step, total)).wait_recv()
            copy(which, step, me).wait_send()
        return 0

    lax.fori_loop(1, total, finish, 0)


def push(arrays, digits, spread, collective_id, name):
    total = math.prod(size for _, _, size in digits)
    vmem = pl.BlockSpec(memory_space=pltpu.VMEM)
    shapes = [a.shape if spread else (total,) + a.shape for a in arrays]
    return pl.pallas_call(
        functools.partial(push_kernel, tuple(digits), spread, len(arrays)),
        in_specs=[vmem] * len(arrays),
        out_specs=[vmem] * len(arrays),
        out_shape=[jax.ShapeDtypeStruct(s, a.dtype) for s, a in zip(shapes, arrays)],
        scratch_shapes=[
            pltpu.SemaphoreType.DMA((len(arrays), total)),
            pltpu.SemaphoreType.DMA((len(arrays), total)),
        ],
        compiler_params=pltpu.CompilerParams(
            collective_id=collective_id, has_side_effects=True, vmem_limit_bytes=VMEM_BYTES // 2
        ),
        name=name,
    )(*arrays)


def shards(
    new_tokens,
    norm_gain,
    w_query,
    w_key,
    w_value,
    w_out,
    pool_keys,
    pool_values,
    cache_lengths,
    owner,
    page_table,
):
    req_count = lax.axis_size("req")
    seq_count = lax.axis_size("seq")
    devices = req_count * seq_count
    req_index = lax.axis_index("req")
    seq_index = lax.axis_index("seq")
    device_index = req_index * seq_count + seq_index
    local_reqs, new_count, model_width = new_tokens.shape
    slot_total = owner.shape[0]
    pages_dev, page_len, kv_width = pool_keys.shape
    pages_req = page_table.shape[1]
    pages_home = pages_req // seq_count
    positions = pages_home * page_len
    per_peer = pages_dev // devices
    query_cols = w_query.shape[1]
    key_cols = w_key.shape[1]
    low_count = 2 if seq_count % 2 == 0 else 1
    high_count = seq_count // low_count
    over_req = [("req", 1, req_count)]
    i32 = jnp.int32
    local_pages = jnp.arange(pages_dev, dtype=i32)

    logical = jnp.arange(pages_req, dtype=i32)[None, :]
    home_index = (
        (owner[:, None] // local_reqs * seq_count + logical // pages_home) * pages_dev
        + owner[:, None] % local_reqs * pages_home
        + logical % pages_home
    )
    held = page_table[None] == (device_index * pages_dev + local_pages)[:, None, None]
    held_homes = jnp.sum(jnp.where(held, home_index[None], 0), axis=(1, 2))
    send_rank = jnp.sum((held_homes[None, :] < held_homes[:, None]).astype(i32), axis=1)
    send_order = jnp.sum(
        jnp.where(send_rank[None, :] == local_pages[:, None], local_pages[None, :], 0), axis=1
    )

    outgoing = collect(send_order, pool_keys, pool_values, devices)
    slots = jnp.arange(slot_total, dtype=i32)
    slot_owned = owner[None, :] == slots[:, None]
    slot_request = jnp.sum(jnp.where(slot_owned, slots[None, :], 0), axis=1)
    slot_lengths = jnp.sum(jnp.where(slot_owned, cache_lengths[None, :], 0), axis=1)
    my_requests = lax.dynamic_slice_in_dim(slot_request, req_index * local_reqs, local_reqs)
    my_lengths = lax.dynamic_slice_in_dim(slot_lengths, req_index * local_reqs, local_reqs)
    seq_pages = lax.dynamic_slice_in_dim(page_table, seq_index * pages_home, pages_home, axis=1)
    is_mine = my_requests[:, None, None] == slots[None, :, None]
    source = jnp.sum(jnp.where(is_mine, seq_pages[None], 0), axis=1).reshape(-1) // pages_dev
    ahead = (source[None, :] == source[:, None]) & (local_pages[None, :] < local_pages[:, None])
    placement = source * (2 * per_peer) + jnp.sum(ahead.astype(i32), axis=1)
    placement = jnp.concatenate([placement, placement + per_peer])

    tokens_wide = new_tokens.astype(jnp.float32)
    square_mean = jnp.mean(tokens_wide * tokens_wide, axis=-1, keepdims=True)
    normed = (tokens_wide * lax.rsqrt(square_mean + NORM_EPS) * norm_gain).astype(jnp.bfloat16)
    normed = normed.reshape(local_reqs * new_count, model_width)
    normed, outgoing = lax.optimization_barrier((normed, outgoing))
    incoming = lax.all_to_all(outgoing, ("req", "seq"), split_axis=0, concat_axis=0, tiled=True)
    incoming = incoming.reshape(2 * pages_dev, page_len, kv_width)
    flat_rows = push([normed], over_req, False, 0, "gather_tokens")[0].reshape(-1, model_width)
    new_index = jnp.arange(new_count, dtype=i32)
    places = slot_lengths[:, None] + new_index[None, :]
    heads = lambda w: jnp.dot(flat_rows, w, preferred_element_type=jnp.float32)
    queries_now = heads(w_query).reshape(slot_total, new_count, query_cols // HD, HD)
    keys_now = heads(w_key).reshape(slot_total, new_count, key_cols // HD, HD)
    queries_now = rotate(queries_now, places).reshape(slot_total * new_count, query_cols)
    keys_now = rotate(keys_now, places).reshape(slot_total * new_count, key_cols)
    projected = jnp.concatenate([queries_now, keys_now, heads(w_value)], axis=-1)
    every = push([projected.astype(jnp.bfloat16)], over_req, False, 1, "gather_heads")[0]
    own_kv = key_cols // HD
    queries = every[..., :query_cols].reshape(
        req_count, slot_total, new_count, own_kv, GROUPS, HD
    )
    queries = jnp.transpose(queries, (0, 3, 1, 4, 2, 5)).reshape(KVH, -1, HD)

    def by_head(part):
        part = part.reshape(req_count, slot_total * new_count, own_kv, HD)
        return jnp.transpose(part, (0, 2, 1, 3)).reshape(KVH, slot_total * new_count, HD)

    def of_mine(part):
        part = part.reshape(req_count, slot_total, new_count, key_cols)
        part = lax.dynamic_slice_in_dim(part, req_index * local_reqs, local_reqs, axis=1)
        part = jnp.transpose(part, (1, 2, 0, 3)).reshape(local_reqs, new_count, kv_width)
        return part.astype(jnp.float32)

    new_keys = every[..., query_cols : query_cols + key_cols]
    new_values = every[..., query_cols + key_cols :]

    held_dev = held_homes // pages_dev
    held_slot = held_dev // seq_count * local_reqs + held_homes % pages_dev // pages_home
    held_first = (held_dev % seq_count * pages_home + held_homes % pages_home) * page_len
    held_length = jnp.sum(
        jnp.where(held_slot[:, None] == slots[None, :], slot_lengths[None, :], 0), axis=1
    )
    spots = held_first[:, None] + jnp.arange(page_len, dtype=i32)[None, :]
    page_info = jnp.where(spots < held_length[:, None], held_slot[:, None], -1).reshape(1, -1)
    own_info = jnp.where(device_index == 0, jnp.repeat(slots, new_count), -1).reshape(1, -1)
    total, peak, mass = attend(
        page_info,
        own_info,
        queries,
        pool_keys.reshape(pages_dev * page_len, kv_width),
        pool_values.reshape(pages_dev * page_len, kv_width),
        by_head(new_keys),
        by_head(new_values),
        new_count,
    )
    peak = peak[..., 0]
    mass = mass[..., 0]
    seq_slots = slot_total // seq_count
    part_rows = seq_slots * GROUPS * new_count

    def by_plane(part):
        part = part.reshape((req_count, own_kv, high_count, low_count, part_rows) + part.shape[2:])
        part = jnp.transpose(part, (0, 3, 2, 1, 4) + tuple(range(5, part.ndim)))
        return part.reshape((req_count * low_count, high_count * own_kv * part_rows) + part.shape[5:])

    def exchange(parts, peaks, masses, digits, spread, collective_id, name):
        count = peaks.shape[-1]
        stats = jnp.stack([peaks, masses], axis=-2)
        wide = ((0, 0),) * (stats.ndim - 2)
        stats = jnp.pad(stats, wide + ((0, 6), (0, -count % HD)))
        parts, stats = push([parts.astype(jnp.bfloat16), stats], digits, spread, collective_id, name)
        peaks = stats[:, 0, :count]
        top = jnp.max(peaks, axis=0)
        rescale = jnp.exp(peaks - top)
        masses = jnp.sum(stats[:, 1, :count] * rescale, axis=0)
        return jnp.sum(parts.astype(jnp.float32) * rescale[..., None], axis=0), top, masses

    plane = [("req", 1, req_count), ("seq", 1, low_count)]
    column = [("seq", low_count, high_count)]
    placing = (placement, my_lengths - seq_index * positions, of_mine(new_keys), of_mine(new_values))
    total, placing = lax.optimization_barrier((total, placing))
    total, peak, mass = exchange(
        by_plane(total), by_plane(peak), by_plane(mass), plane, True, 2, "share_in_plane"
    )
    total, peak, mass = exchange(total, peak, mass, column, False, 5, "share_in_column")
    attended = (total / mass[:, None]).astype(jnp.bfloat16)
    attended = attended.reshape(high_count, own_kv, seq_slots, GROUPS, new_count, HD)
    attended = jnp.transpose(attended, (0, 2, 4, 1, 3, 5)).reshape(-1, query_cols)
    shares = jnp.dot(attended, w_out, preferred_element_type=jnp.float32).astype(jnp.bfloat16)
    shares = shares.reshape(req_count, 1, -1, model_width)
    shares = jnp.broadcast_to(shares, (req_count, low_count) + shares.shape[2:])
    shares = shares.reshape((req_count * low_count,) + shares.shape[2:])
    shares = push([shares], plane, True, 4, "share_outputs")[0]
    shares = shares.reshape(
        req_count, low_count, high_count // req_count, seq_slots * new_count, model_width
    )
    summed = jnp.swapaxes(jnp.sum(shares.astype(jnp.float32), axis=0), 0, 1)
    out_hidden = (tokens_wide + summed.reshape(tokens_wide.shape)).astype(jnp.bfloat16)

    out_shape = (local_reqs, positions, kv_width)
    keys_out, values_out = place(*placing, incoming)
    return (out_hidden, keys_out.reshape(out_shape), values_out.reshape(out_shape))


def solution(mesh):
    return jax.shard_map(
        shards,
        mesh=mesh,
        in_specs=(
            P("req", None, None),
            P(),
            P(None, "req"),
            P(None, "req"),
            P(None, "req"),
            P("req", None),
            P(("req", "seq"), None, None),
            P(("req", "seq"), None, None),
            P(),
            P(),
            P(),
        ),
        out_specs=(P("req", None, None), P("req", "seq", None), P("req", "seq", None)),
        check_vma=False,
    )
```
